128 devices in a mesh: cuts: 4 (over z), dp: 32 (over x, y, core).
Axes of the slice: x: 4, y: 4, z: 4, core: 2. Of those that a mesh axis runs over, the one named last changes fastest.
Arguments:
- hidden: bfloat16 [49152, 8192], P(('cuts', 'dp')), may hold values from -24 to 24
- kv_weight: bfloat16 [8192, 256], P(('cuts', 'dp')), may hold values from -0.0625 to 0.0625
- queries: bfloat16 [49152, 1024], P(('cuts', 'dp')), may hold values from -102 to 102
- out_grad: bfloat16 [49152, 1024], P(('cuts', 'dp')), may hold values from -6 to 6
- lengths: int32 [264], replicated, may hold values from 0 to 1536, as said below
Outputs:
- attended: bfloat16 [49152, 1024], P(('cuts', 'dp'))
- query_grad: bfloat16 [49152, 1024], P(('cuts', 'dp'))
- weight_grad: float32 [8192, 256], P(('cuts', 'dp'))
The draws below stay inside these ranges and needn't reach their ends.
Inputs may be any that keep to these rules, and one draw needn't show every extreme that they name: Taken in order, the entries are the lengths of consecutive documents of the whole stream and sum to 49152; a zero entry is an empty document; the longest document has exactly 1536 tokens.
All inputs are finite; a program needn't handle non-finite values.
Results may differ from the reference program's by a relative error of at most 0.04.
The reference program's roundings to bfloat16 on the way (of `key_value`, `rounded`, `score_grad` and `kv_grad`) count: a program that leaves them out, or rounds other values in their place, can miss the bound.
Values may be sent and summed in bfloat16 or wider, within the bound.
No kernel may reach another device: no remote copies, remote signals or barrier semaphores. Data moves between devices by JAX's collectives and lax.ppermute only.
A program may use at most 128 MiB of HBM per device.

```python
import math
import jax
import jax.numpy as jnp
from jax import lax

D = 8192
HEAD = 128
GROUP = 8
TOK_DEV = 384
SPAN = 4
KCUT = 7
MOST = 1536
TOKENS = 49152
SUPER = 32
N_CUTS = 4
N_DP = 32


def draw_lengths(key, part):
    key = jax.random.fold_in(key, 11)
    first_key, cut_key, count_key, whole_key = jax.random.split(key, 4)
    offset = jax.random.randint(first_key, (), 1, MOST)
    stretch = jnp.concatenate([offset[None], jnp.full((SUPER - 1,), MOST, jnp.int32), (MOST - offset)[None]]).astype(jnp.int32)
    raw_cuts = jax.random.randint(cut_key, (SUPER + 1, KCUT), 0, MOST)
    counts = jax.random.randint(count_key, (SUPER + 1, 1), 1, KCUT + 1)
    slots = jnp.arange(KCUT, dtype=jnp.int32)[None, :]
    raw_cuts = jnp.where(slots < counts, raw_cuts, 0)
    whole = jax.random.randint(whole_key, (), 1, SUPER)
    stretch_ids = jnp.arange(SUPER + 1, dtype=jnp.int32)[:, None]
    raw_cuts = jnp.where(stretch_ids == whole, 0, raw_cuts)
    placed = jnp.sort(raw_cuts * stretch[:, None] // MOST, axis=1)
    bounds = jnp.concatenate([jnp.zeros((SUPER + 1, 1), jnp.int32), placed, stretch[:, None]], axis=1)
    return jnp.diff(bounds, axis=1).reshape(-1).astype(jnp.int32)


def draw_queries(key, part):
    key = jax.random.fold_in(key, 23)
    base_key = jax.random.fold_in(key, 0)
    values = jnp.clip(jax.random.normal(base_key, (TOKENS, GROUP * HEAD), jnp.float32), -4.0, 4.0)
    return values.astype(jnp.bfloat16)


def with_spikes(values, stream_key, source, target, blocks, factor):
    def block_of(axis_at):
        return (jnp.arange(values.shape[axis_at]) // (values.shape[axis_at] // blocks)).reshape((-1,) + (1,) * (values.ndim - 1 - axis_at))

    one_side = jax.random.permutation(stream_key, blocks)[block_of(target)]
    second = (block_of(target) + blocks // 2) % blocks
    return jnp.where((block_of(source) == one_side) | (block_of(source) == second), factor * values, values)


def levels(key, dims, cuts, smallest, top_value):
    def one(position, shards_of):
        draws = jax.random.uniform(jax.random.fold_in(jax.random.fold_in(key, 6), position), (shards_of,), jnp.float32, smallest / len(cuts), top_value / len(cuts))
        return jnp.repeat(jnp.exp(draws), dims[position] // shards_of).reshape((-1,) + (1,) * (len(dims) - position - 1))

    loudness = one(*cuts[0])
    for cut in cuts[1:]:
        loudness = loudness * one(*cut)
    return loudness


def noise(key, extent, spread, limit, pieces=(), kind=jnp.bfloat16):
    level = levels(key, extent, pieces, -0.22, 0.18) if pieces else 1.0
    result = jax.random.normal(key, extent, jnp.float32) * spread * level
    return jnp.minimum(jnp.maximum(result, -limit), limit).astype(kind)


def gaussian_with(rng, shape, deviation, most, cuts, heavy, kind=jnp.bfloat16):
    values = deviation * jax.random.normal(rng, shape, jnp.float32)
    if cuts:
        values = values * levels(rng, shape, cuts, -0.22, 0.18)
    return jnp.clip(with_spikes(values, jax.random.fold_in(rng, 3), *heavy), -most, most).astype(kind)


def setup_inputs(seed: int = 0) -> dict:
    keys = jax.random.split(jax.random.key(seed), 6)
    return {
        "hidden": gaussian_with(keys[0], (TOKENS, D), 1.0, 24.0, ((0, 128),), (0, 1, 128, 5.5)),
        "kv_weight": noise(keys[1], (D, 2 * HEAD), D ** -0.5, 0.0625, ((0, 128),)),
        "queries": draw_queries(jax.random.fold_in(keys[5], 71), 0),
        "out_grad": noise(keys[3], (TOKENS, GROUP * HEAD), 1.0, 6.0, ((0, 128),)),
        "lengths": draw_lengths(jax.random.fold_in(keys[5], 71), 0),
    }


NEG = -1e+30

def segment_ids(lengths, positions):
    doc_ends = jnp.cumsum(lengths).astype(jnp.int32)
    counted = lax.optimization_barrier(jnp.sum((positions[:, None] >= doc_ends[None, :]).astype(jnp.int32), axis=1))
    return jnp.where(positions < 0, -1, counted).astype(jnp.int32)

def attend_block(queried, gradient, key_rows, values, allowed, score_scale):
    wide = jnp.float32
    scores = jnp.einsum('ihd,jd->hij', queried.astype(wide), key_rows.astype(wide)) * score_scale
    scores = jnp.where(allowed[None], scores, NEG)
    row_max = lax.optimization_barrier(jnp.max(scores, axis=2, keepdims=True))
    exponent = jnp.where(allowed[None], jnp.exp(scores - row_max), 0.0)
    weights = exponent / lax.optimization_barrier(jnp.sum(exponent, axis=2, keepdims=True))
    rounded = weights.astype(jnp.bfloat16)
    output = jnp.einsum('hij,jd->ihd', rounded.astype(wide), values.astype(wide))
    row_delta = jnp.transpose(lax.optimization_barrier(jnp.sum(gradient.astype(wide) * output, axis=2)))
    prob_grad = jnp.einsum('ihd,jd->hij', gradient.astype(wide), values.astype(wide))
    score_grad = (weights * (prob_grad - row_delta[:, :, None])).astype(jnp.bfloat16)
    query_part = jnp.einsum('hij,jd->ihd', score_grad.astype(wide), key_rows.astype(wide)) * score_scale
    key_part = jnp.einsum('hij,ihd->jd', score_grad.astype(wide), queried.astype(wide)) * score_scale
    value_part = jnp.einsum('hij,ihd->jd', rounded.astype(wide), gradient.astype(wide))
    return (output.astype(jnp.bfloat16), query_part.astype(jnp.bfloat16), jnp.concatenate([key_part, value_part], axis=1))

def reference(hidden, kv_weight, queries, out_grad, lengths):
    score_scale = 1.0 / math.sqrt(HEAD)
    device_count = N_CUTS * N_DP
    key_value = jnp.dot(hidden, kv_weight, preferred_element_type=jnp.float32).astype(jnp.bfloat16)
    margin = SPAN * TOK_DEV
    window_len = (SPAN + 1) * TOK_DEV
    padded = jnp.concatenate([jnp.zeros((margin, 2 * HEAD), jnp.bfloat16), key_value], axis=0)
    padded_pos = jnp.arange(TOKENS + margin, dtype=jnp.int32) - margin
    padded_seg = segment_ids(lengths, padded_pos)
    grouped_q = queries.reshape(device_count, TOK_DEV, GROUP, HEAD)
    grouped_g = out_grad.reshape(device_count, TOK_DEV, GROUP, HEAD)

    def step(accumulated, inputs):
        block_index, queried, gradient = inputs
        begin_row = (block_index * TOK_DEV).astype(jnp.int32)
        window = lax.dynamic_slice_in_dim(padded, begin_row, window_len, 0)
        key_seg = lax.dynamic_slice_in_dim(padded_seg, begin_row, window_len, 0)
        query_seg = lax.dynamic_slice_in_dim(padded_seg, begin_row + margin, TOK_DEV, 0)
        key_pos = begin_row - margin + jnp.arange(window_len, dtype=jnp.int32)
        query_pos = begin_row + jnp.arange(TOK_DEV, dtype=jnp.int32)
        allowed = (query_seg[:, None] == key_seg[None, :]) & (key_pos[None, :] <= query_pos[:, None])
        output, query_part, kv_part = attend_block(queried, gradient, window[:, :HEAD], window[:, HEAD:], allowed, score_scale)
        current = lax.dynamic_slice_in_dim(accumulated, begin_row, window_len, 0)
        accumulated = lax.dynamic_update_slice_in_dim(accumulated, current + kv_part, begin_row, 0)
        return (accumulated, (output, query_part))
    start_acc = jnp.zeros((TOKENS + margin, 2 * HEAD), jnp.float32)
    indices = jnp.arange(device_count, dtype=jnp.int32)
    accumulated, (outputs, query_parts) = lax.scan(step, start_acc, (indices, grouped_q, grouped_g))
    kv_grad = accumulated[margin:].astype(jnp.bfloat16)
    weight_grad = jnp.dot(hidden.T, kv_grad, preferred_element_type=jnp.float32)
    attended = outputs.reshape(TOKENS, GROUP * HEAD)
    query_grad = query_parts.reshape(TOKENS, GROUP * HEAD)
    return (attended, query_grad, weight_grad)
```

```python
import math

import jax
import jax.numpy as jnp
from jax import lax
from jax.sharding import Mesh, PartitionSpec as P

SPAN = 4
NEG = -1e30
CHIPS = ("z", "x", "y")
ALL = ("z", "x", "y", "core")
SWAP = [(0, 1), (1, 0)]


def passed_along(block, distance):
    devices = range(lax.axis_size(ALL))
    route = [(i - distance, i) for i in devices if i - distance in devices]
    return lax.ppermute(block, ALL, route)


def segment_ids(doc_ends, positions):
    counted = jnp.sum((positions[:, None] >= doc_ends[None, :]).astype(jnp.int32), axis=1)
    return jnp.where(positions < 0, -1, counted)


def gathered_weight(kv_weight):
    chips = lax.axis_size(CHIPS)
    core = lax.axis_index("core")
    copies = jnp.broadcast_to(kv_weight[None], (chips,) + kv_weight.shape)
    mine = lax.all_to_all(copies, CHIPS, 0, 0, tiled=True)
    other = lax.ppermute(mine, "core", SWAP)
    low = jnp.where(core == 0, mine, other)
    high = jnp.where(core == 0, other, mine)
    return jnp.stack([low, high], axis=1).reshape(-1, kv_weight.shape[1])


def summed_over_devices(partial):
    chips = lax.axis_size(CHIPS)
    core = lax.axis_index("core")
    rows, columns = partial.shape
    halves = partial.astype(jnp.bfloat16).reshape(chips, 2, rows // (2 * chips), columns)
    away = lax.dynamic_index_in_dim(halves, 1 - core, 1, keepdims=False)
    keep = lax.dynamic_index_in_dim(halves, core, 1, keepdims=False)
    came = lax.ppermute(away, "core", SWAP)
    both = (keep.astype(jnp.float32) + came.astype(jnp.float32)).astype(jnp.bfloat16)
    spread = lax.all_to_all(both, CHIPS, 0, 0, tiled=True)
    return jnp.sum(spread.astype(jnp.float32), axis=0)


def per_device(hidden, kv_weight, queries, out_grad, lengths):
    row_count = hidden.shape[0]
    pair_width = kv_weight.shape[1]
    head_size = pair_width // 2
    query_heads = queries.shape[1] // head_size
    score_scale = 1.0 / math.sqrt(head_size)
    projected = jnp.dot(hidden, gathered_weight(kv_weight), preferred_element_type=jnp.float32)
    key_value = projected.astype(jnp.bfloat16)
    pieces = [key_value]
    for distance in range(1, SPAN + 1):
        pieces.append(passed_along(key_value, distance))
    window = jnp.concatenate(pieces[::-1], axis=0)
    offset = lax.axis_index(ALL) * row_count
    doc_ends = jnp.cumsum(lengths)
    query_pos = offset + jnp.arange(row_count, dtype=jnp.int32)
    query_seg = segment_ids(doc_ends, query_pos)
    queried = queries.reshape(row_count, query_heads, head_size)
    gradient = out_grad.reshape(row_count, query_heads, head_size)

    def view(number):
        start_row = number * row_count
        key_rows = window[start_row : start_row + row_count, :head_size]
        values = window[start_row : start_row + row_count, head_size:]
        key_pos = offset - SPAN * row_count + start_row + jnp.arange(row_count, dtype=jnp.int32)
        key_seg = segment_ids(doc_ends, key_pos)
        allowed = (query_seg[:, None] == key_seg[None, :]) & (
            key_pos[None, :] <= query_pos[:, None]
        )
        return (key_rows, values, allowed)

    def masked_scores(key_rows, allowed):
        scores = (
            jnp.einsum("ihd,jd->hij", queried, key_rows, preferred_element_type=jnp.float32)
            * score_scale
        )
        return jnp.where(allowed[None], scores, NEG)

    blocks = [view(number) for number in range(SPAN + 1)]
    running = (
        jnp.full((query_heads, row_count), NEG, jnp.float32),
        jnp.zeros((query_heads, row_count), jnp.float32),
    )
    for key_rows, values, allowed in blocks:
        stats_row_max, stats_row_sum = running
        stats_scores = masked_scores(key_rows, allowed)
        new_max = jnp.maximum(stats_row_max, jnp.max(stats_scores, axis=2))
        stats_exponent = jnp.where(allowed[None], jnp.exp(stats_scores - new_max[:, :, None]), 0.0)
        running = (
            new_max,
            stats_row_sum * jnp.exp(stats_row_max - new_max) + jnp.sum(stats_exponent, axis=2),
        )
    row_max, row_sum = running

    def probabilities(key_rows, allowed):
        scores = masked_scores(key_rows, allowed)
        exponent = jnp.where(allowed[None], jnp.exp(scores - row_max[:, :, None]), 0.0)
        return exponent / row_sum[:, :, None]

    output = jnp.zeros((row_count, query_heads, head_size), jnp.float32)
    for key_rows, values, allowed in blocks:
        output_rounded = probabilities(key_rows, allowed).astype(jnp.bfloat16)
        output = output + jnp.einsum(
            "hij,jd->ihd", output_rounded, values, preferred_element_type=jnp.float32
        )
    attended = output.astype(jnp.bfloat16)
    row_delta = jnp.transpose(jnp.sum(gradient.astype(jnp.float32) * output, axis=2))
    query_sum = jnp.zeros((row_count, query_heads, head_size), jnp.float32)
    block_grads = []
    for key_rows, values, allowed in blocks:
        weights = probabilities(key_rows, allowed)
        rounded = weights.astype(jnp.bfloat16)
        prob_grad = jnp.einsum("ihd,jd->hij", gradient, values, preferred_element_type=jnp.float32)
        score_grad = (weights * (prob_grad - row_delta[:, :, None])).astype(jnp.bfloat16)
        query_sum = query_sum + jnp.einsum(
            "hij,jd->ihd", score_grad, key_rows, preferred_element_type=jnp.float32
        )
        key_part = (
            jnp.einsum("hij,ihd->jd", score_grad, queried, preferred_element_type=jnp.float32)
            * score_scale
        )
        value_part = jnp.einsum(
            "hij,ihd->jd", rounded, gradient, preferred_element_type=jnp.float32
        )
        block_grads.append(jnp.concatenate([key_part, value_part], axis=1))
    query_grad = (
        (query_sum * score_scale).astype(jnp.bfloat16).reshape(row_count, query_heads * head_size)
    )
    summed = block_grads[SPAN]
    for distance in range(1, SPAN + 1):
        sent = block_grads[SPAN - distance].astype(jnp.bfloat16)
        summed = summed + passed_along(sent, -distance).astype(jnp.float32)
    kv_grad = summed.astype(jnp.bfloat16)
    partial = lax.dot_general(
        hidden, kv_grad, (((0,), (0,)), ((), ())), preferred_element_type=jnp.float32
    )
    weight_grad = summed_over_devices(partial)
    return (attended.reshape(row_count, query_heads * head_size), query_grad, weight_grad)


def solution(mesh):
    cuts, dp = mesh.devices.shape
    fine = Mesh(mesh.devices.reshape(cuts, 4, dp // 8, 2), ALL)
    rows = P(ALL, None)
    return jax.shard_map(
        per_device,
        mesh=fine,
        in_specs=(rows, rows, rows, rows, P()),
        out_specs=(rows, rows, rows),
        check_vma=False,
    )
```

```python
import functools
import math

import jax
import jax.numpy as jnp
from jax import lax
from jax.experimental import pallas as pl
from jax.experimental.pallas import tpu as pltpu
from jax.sharding import Mesh, PartitionSpec as P

SPAN = 4
NEG = -1e30
CHIPS = ("z", "x", "y")
ALL = ("z", "x", "y", "core")
SWAP = [(0, 1), (1, 0)]
CHUNKS = 4
VMEM = 56 * 1024 * 1024
BF = jnp.bfloat16
F32 = jnp.float32


def mm(a, b):
    return jnp.dot(a, b, preferred_element_type=F32)


def away_kernel(pick_ref, x_ref, away_ref):
    for n in range(x_ref.shape[1] // 256):
        y = mm(x_ref[:, n * 256 : (n + 1) * 256], pick_ref[...])
        away_ref[:, n * 128 : (n + 1) * 128] = y.astype(BF)


def keep_kernel(pick_ref, x_ref, keep_ref, turned_ref):
    for n in range(x_ref.shape[1] // 256):
        y = mm(x_ref[:, n * 256 : (n + 1) * 256], pick_ref[...]).astype(BF)
        keep_ref[:, n * 128 : (n + 1) * 128] = y
        turned_ref[n * 128 : (n + 1) * 128, :] = y.T


def join_kernel(*refs):
    parts, (whole_ref, turned_ref) = refs[:-2], refs[-2:]
    at = 0
    for part in parts:
        for n in range(0, part.shape[1], 128):
            y = part[:, n : n + 128]
            whole_ref[:, at : at + 128] = y
            turned_ref[at : at + 128, :] = y.T
            at += 128


def share_kernel(keep_ref, came_ref, mine_ref, other_ref, share_ref):
    share_ref[...] = (mm(keep_ref[...], mine_ref[...]) + mm(came_ref[...], other_ref[...])).astype(BF)


def params():
    return pltpu.CompilerParams(vmem_limit_bytes=VMEM)


def picker(side, part):
    out = jnp.arange(128, dtype=jnp.int32)
    source = (out // part) * 2 * part + side * part + out % part
    return (jnp.arange(256, dtype=jnp.int32)[:, None] == source[None, :]).astype(BF)


def away_columns(hidden, pick, chunk, chunks):
    rows, width = hidden.shape
    block = width // (2 * chunks)
    return pl.pallas_call(
        away_kernel,
        grid=(2,),
        in_specs=[
            pl.BlockSpec((256, 128), lambda i: (0, 0)),
            pl.BlockSpec((rows, block), lambda i: (0, 2 * chunk + i)),
        ],
        out_specs=pl.BlockSpec((rows, block // 2), lambda i: (0, i)),
        out_shape=jax.ShapeDtypeStruct((rows, block), BF),
        cost_estimate=pl.CostEstimate(flops=0, bytes_accessed=6 * rows * block, transcendentals=0),
        compiler_params=params(),
        name="away_columns",
    )(pick, hidden)


def kept_columns(hidden, pick):
    rows, width = hidden.shape
    block = 1024
    return pl.pallas_call(
        keep_kernel,
        grid=(width // block,),
        in_specs=[
            pl.BlockSpec((256, 128), lambda i: (0, 0)),
            pl.BlockSpec((rows, block), lambda i: (0, i)),
        ],
        out_specs=[
            pl.BlockSpec((rows, block // 2), lambda i: (0, i)),
            pl.BlockSpec((block // 2, rows), lambda i: (i, 0)),
        ],
        out_shape=[jax.ShapeDtypeStruct((rows, width // 2), BF), jax.ShapeDtypeStruct((width // 2, rows), BF)],
        cost_estimate=pl.CostEstimate(flops=0, bytes_accessed=6 * rows * width, transcendentals=0),
        compiler_params=params(),
        name="kept_columns",
    )(pick, hidden)


def joined(parts):
    rows, width = parts[0].shape[0], sum(part.shape[1] for part in parts)
    return pl.pallas_call(
        join_kernel,
        out_shape=[jax.ShapeDtypeStruct((rows, width), BF), jax.ShapeDtypeStruct((width, rows), BF)],
        cost_estimate=pl.CostEstimate(flops=0, bytes_accessed=8 * rows * width, transcendentals=0),
        compiler_params=params(),
        name="joined",
    )(*parts)


def chip_share(keep_t, came_t, mine, other):
    height, rows = keep_t.shape
    pair = mine.shape[1]
    block = 512
    return pl.pallas_call(
        share_kernel,
        grid=(height // block,),
        in_specs=[
            pl.BlockSpec((block, rows), lambda i: (i, 0)),
            pl.BlockSpec((block, rows), lambda i: (i, 0)),
            pl.BlockSpec((rows, pair), lambda i: (0, 0)),
            pl.BlockSpec((rows, pair), lambda i: (0, 0)),
        ],
        out_specs=pl.BlockSpec((block, pair), lambda i: (i, 0)),
        out_shape=jax.ShapeDtypeStruct((height, pair), BF),
        cost_estimate=pl.CostEstimate(flops=4 * height * rows * pair, bytes_accessed=6 * height * rows, transcendentals=0),
        compiler_params=params(),
        name="chip_share",
    )(keep_t, came_t, mine, other)


def key_chunks(rows):
    edge, span = 2 * rows // 3, (SPAN + 1) * rows
    chunks = [(0, edge, 0, edge)]
    at = edge
    while at < span - edge:
        end = min(at + 768, span - edge)
        chunks.append((at, end, 0, rows))
        at = end
    chunks.append((span - edge, span, rows - edge, rows))
    return chunks


def onto_rows(total, extra, first, end):
    parts = [total[:first], total[first:end] + extra, total[end:]]
    return jnp.concatenate([part for part in parts if part.shape[0]], axis=0)


def lane_groups(block, size):
    return [block[:, n : n + size] for n in range(0, block.shape[1], size)]


def attention_kernel(low_ref, q_ref, g_ref, *refs):
    pieces = refs[: SPAN + 1]
    out_ref, dq_ref, swap_ref, rest_ref, kv_ref, turned_ref, bias_ref, s_ref, p_ref, acc_ref = refs[SPAN + 1 :]
    step = pl.program_id(0)
    rows = q_ref.shape[0]
    size = kv_ref.shape[1] // 2
    span = kv_ref.shape[0]
    chunks = key_chunks(rows)
    scale = 1.0 / math.sqrt(size)
    scale2 = scale * math.log2(math.e)

    @pl.when(step == 0)
    def _():
        low = low_ref[:, :1]
        row = lax.broadcasted_iota(jnp.int32, (rows, rows), 0)
        for j, piece in enumerate(pieces):
            cols = slice(j * rows, (j + 1) * rows)
            kv_ref[cols, :] = piece[...]
            turned_ref[:size, cols] = piece[:, :size].T
            turned_ref[size:, cols] = piece[:, size:].T
            at = lax.broadcasted_iota(jnp.int32, (rows, rows), 1) + j * rows
            allowed = (at >= low) & (at <= row + SPAN * rows)
            bias_ref[:, cols] = jnp.where(allowed, 0.0, NEG)
        acc_ref[...] = jnp.zeros_like(acc_ref)

    heads = q_ref.shape[1] // size
    for h in range(heads):
        lanes = slice(h * size, (h + 1) * size)
        q = q_ref[:, lanes]
        top = jnp.full((rows, size), NEG, F32)
        for c0, c1, r0, r1 in chunks:
            s = mm(q[r0:r1], turned_ref[:size, c0:c1]) + bias_ref[r0:r1, c0:c1]
            s_ref[h, r0:r1, c0:c1] = s
            most = functools.reduce(jnp.maximum, lane_groups(s, size))
            parts = [top[:r0], jnp.maximum(top[r0:r1], most), top[r1:]]
            top = jnp.concatenate([part for part in parts if part.shape[0]], axis=0)
        peak = jnp.max(top, axis=1, keepdims=True) * scale2
        total = jnp.zeros((rows, size), F32)
        out = jnp.zeros((rows, size), F32)
        for c0, c1, r0, r1 in chunks:
            e = jnp.exp2(s_ref[h, r0:r1, c0:c1] * scale2 - peak[r0:r1])
            total = onto_rows(total, functools.reduce(jnp.add, lane_groups(e, size)), r0, r1)
            p = e.astype(BF)
            p_ref[h, r0:r1, c0:c1] = p
            out = onto_rows(out, mm(p, kv_ref[c0:c1, size:]), r0, r1)
        inverse = 1.0 / jnp.sum(total, axis=1, keepdims=True)
        out = out * inverse
        out_ref[:, lanes] = out.astype(BF)
        scaled = g_ref[:, lanes].astype(F32) * inverse
        g = scaled.astype(BF)
        delta = jnp.sum(g.astype(F32) * out, axis=1, keepdims=True)
        g_turned = scaled.T.astype(BF)
        q_turned = q.astype(F32).T.astype(BF)
        dq = jnp.zeros((rows, size), F32)
        for c0, c1, r0, r1 in chunks:
            p = p_ref[h, r0:r1, c0:c1]
            acc_ref[size:, c0:c1] += mm(g_turned[:, r0:r1], p)
            dp = mm(g[r0:r1], turned_ref[size:, c0:c1]) - delta[r0:r1]
            ds = dp.astype(BF) * p
            dq = onto_rows(dq, mm(ds, kv_ref[c0:c1, :size]), r0, r1)
            acc_ref[:size, c0:c1] += mm(q_turned[:, r0:r1], ds)
        dq_ref[:, lanes] = (dq * scale).astype(BF)

    @pl.when(step == pl.num_programs(0) - 1)
    def _():
        for j in range(SPAN + 1):
            cols = slice(j * rows, (j + 1) * rows)
            into = rest_ref.at[j // 2] if j % 2 == 0 else swap_ref.at[1 - j // 2]
            into[:, :size] = (acc_ref[:size, cols].T * scale).astype(BF)
            into[:, size:] = acc_ref[size:, cols].T.astype(BF)


HEADS_PER_STEP = 2


def attention(low, queries, out_grad, pieces):
    rows, width = queries.shape
    pair = pieces[0].shape[1]
    size = pair // 2
    heads = width // size
    span = (SPAN + 1) * rows
    several = pl.BlockSpec((rows, HEADS_PER_STEP * size), lambda h: (0, h))
    whole = pl.BlockSpec((rows, pair), lambda h: (0, 0))
    return pl.pallas_call(
        attention_kernel,
        grid=(heads // HEADS_PER_STEP,),
        in_specs=[pl.BlockSpec((rows, size), lambda h: (0, 0)), several, several] + [whole] * (SPAN + 1),
        out_specs=[
            several,
            several,
            pl.BlockSpec((SPAN // 2, rows, pair), lambda h: (0, 0, 0)),
            pl.BlockSpec((SPAN // 2 + 1, rows, pair), lambda h: (0, 0, 0)),
        ],
        out_shape=[
            jax.ShapeDtypeStruct((rows, width), BF),
            jax.ShapeDtypeStruct((rows, width), BF),
            jax.ShapeDtypeStruct((SPAN // 2, rows, pair), BF),
            jax.ShapeDtypeStruct((SPAN // 2 + 1, rows, pair), BF),
        ],
        scratch_shapes=[
            pltpu.VMEM((span, pair), BF),
            pltpu.VMEM((pair, span), BF),
            pltpu.VMEM((rows, span), F32),
            pltpu.VMEM((HEADS_PER_STEP, rows, span), F32),
            pltpu.VMEM((HEADS_PER_STEP, rows, span), BF),
            pltpu.VMEM((pair, span), F32),
        ],
        cost_estimate=pl.CostEstimate(
            flops=24 * heads * rows * span * size, bytes_accessed=10 * rows * width, transcendentals=heads * rows * span
        ),
        compiler_params=params(),
        name="attention",
    )(low, queries, out_grad, *pieces)


def between_cores(block):
    return lax.ppermute(block, "core", SWAP)


def between_chips(block, distance):
    devices = range(lax.axis_size(ALL))
    route = [(i, i + 2 * distance) for i in devices if i + 2 * distance in devices]
    return lax.ppermute(block, ALL, route)


def window_pieces(key_value, core):
    second = between_chips(key_value, 1)
    fourth = between_chips(key_value, 2)
    first = between_cores(jnp.where(core == 0, key_value, second))
    third = between_cores(jnp.where(core == 0, second, fourth))
    return [fourth, third, second, first, key_value]


def returned(swap, rest, core):
    came = between_cores(swap)
    first, third = came[0].astype(F32), came[1].astype(F32)
    near = (rest[1].astype(F32) + jnp.where(core == 0, third, first)).astype(BF)
    far = (rest[0].astype(F32) + jnp.where(core == 0, 0.0, third)).astype(BF)
    own = rest[2].astype(F32) + jnp.where(core == 0, first, 0.0)
    summed = own + between_chips(near, -1).astype(F32) + between_chips(far, -2).astype(F32)
    mine = summed.astype(BF)
    return mine, between_cores(mine)


def per_device(hidden, kv_weight, queries, out_grad, lengths):
    rows = hidden.shape[0]
    part, pair = kv_weight.shape
    core = lax.axis_index("core")
    chips = lax.axis_size(CHIPS)

    copies = jnp.broadcast_to(kv_weight[None], (chips, part, pair))
    weight = lax.all_to_all(copies, CHIPS, 0, 0, tiled=True).reshape(chips * part, pair)

    away = picker(1 - core, part)
    came, came_t = joined([between_cores(away_columns(hidden, away, n, CHUNKS)) for n in range(CHUNKS)])
    keep, keep_t = kept_columns(hidden, picker(core, part))

    offset = lax.axis_index(ALL) * rows
    position = offset + jnp.arange(rows, dtype=jnp.int32)
    ends = jnp.cumsum(lengths)
    start = jnp.max(jnp.where(ends[None, :] <= position[:, None], ends[None, :], 0), axis=1)
    low = (start - (offset - SPAN * rows)).astype(jnp.int32)
    low = jnp.broadcast_to(low[:, None], (rows, pair // 2))

    partner = between_cores(mm(came, weight))
    key_value = (mm(keep, weight) + partner).astype(BF)
    pieces = window_pieces(key_value, core)

    attended, query_grad, swap, rest = attention(low, queries, out_grad, pieces)
    mine, other = returned(swap, rest, core)
    share = chip_share(keep_t, came_t, mine, other).reshape(chips, part, pair)
    spread = lax.all_to_all(share, CHIPS, 0, 0, tiled=True)
    return attended, query_grad, jnp.sum(spread.astype(F32), axis=0)


def solution(mesh):
    cuts, dp = mesh.devices.shape
    fine = Mesh(mesh.devices.reshape(cuts, 4, dp // 8, 2), ALL)
    rows = P(ALL, None)
    return jax.shard_map(
        per_device,
        mesh=fine,
        in_specs=(rows, rows, rows, rows, P()),
        out_specs=(rows, rows, rows),
        check_vma=False,
    )
```

```python
import functools
import math

import jax
import jax.numpy as jnp
from jax import lax
from jax.experimental import pallas as pl
from jax.experimental.pallas import tpu as pltpu
from jax.sharding import Mesh, PartitionSpec as P

SPAN = 4
PIECES = 6
NEG = -1e30
CHIPS = ("z", "x", "y")
ALL = ("z", "x", "y", "core")
SWAP = [(0, 1), (1, 0)]
CHUNKS = 4
BF = jnp.bfloat16
F32 = jnp.float32


def mm(a, b):
    return jnp.dot(a, b, preferred_element_type=F32)


def pick_kernel(pick_ref, x_ref, out_ref):
    for n in range(x_ref.shape[1] // 256):
        y = mm(x_ref[:, n * 256 : (n + 1) * 256], pick_ref[...])
        out_ref[:, n * 128 : (n + 1) * 128] = y.astype(BF)


def across(a, b):
    return lax.dot_general(a, b, (((0,), (0,)), ((), ())), preferred_element_type=F32)


def share_kernel(*refs):
    chunks = (len(refs) - 3) // 2
    mine_ref, other_ref, share_ref = refs[-3:]
    for n in range(chunks):
        both = across(refs[n][...], mine_ref[...]) + across(refs[chunks + n][...], other_ref[...])
        share_ref[n] = both.astype(BF)


def project_kernel(*refs):
    parts, (weight_ref, out_ref) = refs[:-2], refs[-2:]
    width = parts[0].shape[1]
    out_ref[...] = sum(mm(part[...], weight_ref[n * width : (n + 1) * width, :]) for n, part in enumerate(parts))


def params(mib=56):
    return pltpu.CompilerParams(vmem_limit_bytes=mib * 1024 * 1024)


def picker(side, part):
    out = jnp.arange(128, dtype=jnp.int32)
    source = (out // part) * 2 * part + side * part + out % part
    return (jnp.arange(256, dtype=jnp.int32)[:, None] == source[None, :]).astype(BF)


def picked_columns(hidden, pick, chunk, chunks):
    rows, width = hidden.shape
    block = 1024
    steps = width // (block * chunks)
    return pl.pallas_call(
        pick_kernel,
        grid=(steps,),
        in_specs=[
            pl.BlockSpec((256, 128), lambda i: (0, 0)),
            pl.BlockSpec((rows, block), lambda i: (0, steps * chunk + i)),
        ],
        out_specs=pl.BlockSpec((rows, block // 2), lambda i: (0, i)),
        out_shape=jax.ShapeDtypeStruct((rows, steps * block // 2), BF),
        cost_estimate=pl.CostEstimate(flops=0, bytes_accessed=3 * rows * block * steps, transcendentals=0),
        compiler_params=params(),
        name="picked_columns",
    )(pick, hidden)


def chip_share(keep, came, mine, other):
    rows, width = keep.shape
    pair = mine.shape[1]
    chunks = len(came)
    block = width // (2 * chunks)
    whole = pl.BlockSpec((rows, pair), lambda i: (0, 0))
    return pl.pallas_call(
        share_kernel,
        grid=(2,),
        in_specs=[pl.BlockSpec((rows, block), lambda i, n=n: (0, 2 * n + i)) for n in range(chunks)]
        + [pl.BlockSpec((rows, block), lambda i: (0, i))] * chunks
        + [whole, whole],
        out_specs=pl.BlockSpec((chunks, block, pair), lambda i: (0, i, 0)),
        out_shape=jax.ShapeDtypeStruct((chunks, 2 * block, pair), BF),
        cost_estimate=pl.CostEstimate(flops=4 * width * rows * pair, bytes_accessed=6 * width * rows, transcendentals=0),
        compiler_params=params(),
        name="chip_share",
    )(*([keep] * chunks), *came, mine, other)


def projected(came, weight):
    rows, pair = came[0].shape[0], weight.shape[1]
    return pl.pallas_call(
        project_kernel,
        out_shape=jax.ShapeDtypeStruct((rows, pair), F32),
        cost_estimate=pl.CostEstimate(flops=2 * rows * weight.size, bytes_accessed=2 * weight.size, transcendentals=0),
        compiler_params=params(16),
        name="projected",
    )(*came, weight)


def key_chunks(rows):
    edge, span = 2 * rows // 3, (SPAN + 1) * rows
    chunks = [(0, edge, 0, edge)]
    at = edge
    while at < span - edge:
        end = min(at + 768, span - edge)
        chunks.append((at, end, 0, rows))
        at = end
    chunks.append((span - edge, span, rows - edge, rows))
    return chunks


def onto_rows(total, extra, first, end):
    parts = [total[:first], total[first:end] + extra, total[end:]]
    return jnp.concatenate([part for part in parts if part.shape[0]], axis=0)


def lane_groups(block, size):
    return [block[:, n : n + size] for n in range(0, block.shape[1], size)]


def attention_kernel(place_ref, ends_ref, q_ref, g_ref, *refs):
    pieces = refs[:PIECES]
    out_ref, dq_ref, swap_ref, rest_ref, kv_ref, turned_ref, bias_ref, s_ref, p_ref, acc_ref = refs[PIECES:]
    step = pl.program_id(0)
    rows = q_ref.shape[0]
    size = kv_ref.shape[1] // 2
    span = kv_ref.shape[0]
    chunks = key_chunks(rows)
    scale = 1.0 / math.sqrt(size)
    scale2 = scale * math.log2(math.e)

    @pl.when(step == 0)
    def _():
        offset, core, ends = place_ref[0], place_ref[1], ends_ref[...]
        position = offset + lax.broadcasted_iota(jnp.int32, (rows, ends.shape[1]), 0)
        start = jnp.max(jnp.where(ends <= position, ends, 0), axis=1, keepdims=True)
        low = start - (offset - SPAN * rows)
        row = lax.broadcasted_iota(jnp.int32, (rows, rows), 0)
        own, second, fourth, other_own, other_second, other_fourth = [piece[...] for piece in pieces]
        first = jnp.where(core == 0, other_second, other_own)
        third = jnp.where(core == 0, other_fourth, other_second)
        for j, piece in enumerate([fourth, third, second, first, own]):
            cols = slice(j * rows, (j + 1) * rows)
            kv_ref[cols, :] = piece
            turned_ref[:size, cols] = piece[:, :size].T
            turned_ref[size:, cols] = piece[:, size:].T
            at = lax.broadcasted_iota(jnp.int32, (rows, rows), 1) + j * rows
            allowed = (at >= low) & (at <= row + SPAN * rows)
            bias_ref[:, cols] = jnp.where(allowed, 0.0, NEG)
        acc_ref[...] = jnp.zeros_like(acc_ref)

    def one_head(h):
        lanes = slice(h * size, (h + 1) * size)
        q = q_ref[:, lanes]
        top = jnp.full((rows, size), NEG, F32)
        for c0, c1, r0, r1 in chunks:
            s = mm(q[r0:r1], turned_ref[:size, c0:c1]) + bias_ref[r0:r1, c0:c1]
            s_ref[h % 2, r0:r1, c0:c1] = s
            most = functools.reduce(jnp.maximum, lane_groups(s, size))
            parts = [top[:r0], jnp.maximum(top[r0:r1], most), top[r1:]]
            top = jnp.concatenate([part for part in parts if part.shape[0]], axis=0)
            yield
        peak = jnp.max(top, axis=1, keepdims=True) * scale2
        total = jnp.zeros((rows, size), F32)
        out = jnp.zeros((rows, size), F32)
        for c0, c1, r0, r1 in chunks:
            e = jnp.exp2(s_ref[h % 2, r0:r1, c0:c1] * scale2 - peak[r0:r1])
            total = onto_rows(total, functools.reduce(jnp.add, lane_groups(e, size)), r0, r1)
            p = e.astype(BF)
            p_ref[h % 2, r0:r1, c0:c1] = p
            out = onto_rows(out, mm(p, kv_ref[c0:c1, size:]), r0, r1)
            yield
        inverse = 1.0 / jnp.sum(total, axis=1, keepdims=True)
        out = out * inverse
        out_ref[:, lanes] = out.astype(BF)
        scaled = g_ref[:, lanes].astype(F32) * inverse
        g = scaled.astype(BF)
        delta = jnp.sum(g.astype(F32) * out, axis=1, keepdims=True)
        g_turned = scaled.T.astype(BF)
        q_turned = q.astype(F32).T.astype(BF)
        dq = jnp.zeros((rows, size), F32)
        for c0, c1, r0, r1 in chunks:
            p = p_ref[h % 2, r0:r1, c0:c1]
            acc_ref[size:, c0:c1] += mm(g_turned[:, r0:r1], p)
            dp = mm(g[r0:r1], turned_ref[size:, c0:c1]) - delta[r0:r1]
            ds = dp.astype(BF) * p
            dq = onto_rows(dq, mm(ds, kv_ref[c0:c1, :size]), r0, r1)
            acc_ref[:size, c0:c1] += mm(q_turned[:, r0:r1], ds)
            yield
        dq_ref[:, lanes] = (dq * scale).astype(BF)

    running, waiting = [], [one_head(h) for h in range(q_ref.shape[1] // size)]
    while running or waiting:
        if waiting:
            running.append(waiting.pop(0))
        for _ in chunks:
            running = [head for head in running if next(head, head) is None]

    @pl.when(step == pl.num_programs(0) - 1)
    def _():
        for j in range(SPAN + 1):
            cols = slice(j * rows, (j + 1) * rows)
            into = rest_ref.at[j // 2] if j % 2 == 0 else swap_ref.at[1 - j // 2]
            into[:, :size] = (acc_ref[:size, cols].T * scale).astype(BF)
            into[:, size:] = acc_ref[size:, cols].T.astype(BF)


HEADS_PER_STEP = 4


def attention(place, ends, queries, out_grad, pieces):
    rows, width = queries.shape
    pair = pieces[0].shape[1]
    size = pair // 2
    heads = width // size
    span = (SPAN + 1) * rows
    several = pl.BlockSpec((rows, HEADS_PER_STEP * size), lambda h: (0, h))
    whole = pl.BlockSpec((rows, pair), lambda h: (0, 0))
    return pl.pallas_call(
        attention_kernel,
        grid=(heads // HEADS_PER_STEP,),
        in_specs=[
            pl.BlockSpec(memory_space=pltpu.SMEM),
            pl.BlockSpec((1, ends.shape[1]), lambda h: (0, 0)),
            several,
            several,
        ]
        + [whole] * PIECES,
        out_specs=[
            several,
            several,
            pl.BlockSpec((SPAN // 2, rows, pair), lambda h: (0, 0, 0)),
            pl.BlockSpec((SPAN // 2 + 1, rows, pair), lambda h: (0, 0, 0)),
        ],
        out_shape=[
            jax.ShapeDtypeStruct((rows, width), BF),
            jax.ShapeDtypeStruct((rows, width), BF),
            jax.ShapeDtypeStruct((SPAN // 2, rows, pair), BF),
            jax.ShapeDtypeStruct((SPAN // 2 + 1, rows, pair), BF),
        ],
        scratch_shapes=[
            pltpu.VMEM((span, pair), BF),
            pltpu.VMEM((pair, span), BF),
            pltpu.VMEM((rows, span), F32),
            pltpu.VMEM((2, rows, span), F32),
            pltpu.VMEM((2, rows, span), BF),
            pltpu.VMEM((pair, span), F32),
        ],
        cost_estimate=pl.CostEstimate(
            flops=24 * heads * rows * span * size, bytes_accessed=10 * rows * width, transcendentals=heads * rows * span
        ),
        compiler_params=params(56),
        name="attention",
    )(place, ends, queries, out_grad, *pieces)


def between_cores(block):
    return lax.ppermute(block, "core", SWAP)


def between_chips(block, distance):
    devices = range(lax.axis_size(ALL))
    route = [(i, i + 2 * distance) for i in devices if i + 2 * distance in devices]
    return lax.ppermute(block, ALL, route)


def window_pieces(key_value):
    second = between_chips(key_value, 1)
    fourth = between_chips(key_value, 2)
    mine = [key_value, second, fourth]
    return mine + [between_cores(block) for block in mine]


def returned(swap, rest, core):
    came = between_cores(swap)
    first, third = came[0].astype(F32), came[1].astype(F32)
    near = (rest[1].astype(F32) + jnp.where(core == 0, third, first)).astype(BF)
    far = (rest[0].astype(F32) + jnp.where(core == 0, 0.0, third)).astype(BF)
    own = rest[2].astype(F32) + jnp.where(core == 0, first, 0.0)
    summed = own + between_chips(near, -1).astype(F32) + between_chips(far, -2).astype(F32)
    mine = summed.astype(BF)
    return mine, between_cores(mine)


def per_device(hidden, kv_weight, queries, out_grad, lengths):
    rows = hidden.shape[0]
    part, pair = kv_weight.shape
    core = lax.axis_index("core")
    chips = lax.axis_size(CHIPS)

    copies = jnp.broadcast_to(kv_weight[None], (chips, part, pair))
    weight = lax.all_to_all(copies, CHIPS, 0, 0, tiled=True).reshape(chips * part, pair)

    away = picker(1 - core, part)
    came = [between_cores(picked_columns(hidden, away, n, CHUNKS)) for n in range(CHUNKS)]
    keep = picked_columns(hidden, picker(core, part), 0, 1)

    place = jnp.stack([lax.axis_index(ALL) * rows, core]).astype(jnp.int32)
    ends = jnp.cumsum(lengths).astype(jnp.int32)[None, :]

    place, ends, keep = lax.optimization_barrier((place, ends, keep))
    partner = between_cores(projected(came, weight))
    key_value = (mm(keep, weight) + partner).astype(BF)
    pieces = window_pieces(key_value)

    attended, query_grad, swap, rest = attention(place, ends, queries, out_grad, pieces)
    mine, other = returned(swap, rest, core)
    share = chip_share(keep, came, mine, other).reshape(chips, part, pair)
    spread = lax.all_to_all(share, CHIPS, 0, 0, tiled=True)
    return attended, query_grad, jnp.sum(spread.astype(F32), axis=0)


def solution(mesh):
    cuts, dp = mesh.devices.shape
    fine = Mesh(mesh.devices.reshape(cuts, 4, dp // 8, 2), ALL)
    rows = P(ALL, None)
    return jax.shard_map(
        per_device,
        mesh=fine,
        in_specs=(rows, rows, rows, rows, P()),
        out_specs=(rows, rows, rows),
        check_vma=False,
    )
```

```python
import functools
import math

import jax
import jax.numpy as jnp
from jax import lax
from jax.experimental import pallas as pl
from jax.experimental.pallas import tpu as pltpu
from jax.sharding import Mesh, PartitionSpec as P

SPAN = 4
PIECES = 6
NEG = -1e30
CHIPS = ("z", "x", "y")
ALL = ("z", "x", "y", "core")
SWAP = [(0, 1), (1, 0)]
CHUNKS = 4
BF = jnp.bfloat16
F32 = jnp.float32


def mm(a, b):
    return jnp.dot(a, b, preferred_element_type=F32)


def pick_kernel(pick_ref, x_ref, out_ref):
    for n in range(x_ref.shape[1] // 256):
        y = mm(x_ref[:, n * 256 : (n + 1) * 256], pick_ref[...])
        out_ref[:, n * 128 : (n + 1) * 128] = y.astype(BF)


def across(a, b):
    return lax.dot_general(a, b, (((0,), (0,)), ((), ())), preferred_element_type=F32)


def share_kernel(*refs):
    chunks = (len(refs) - 9) // 2
    terms, (share_ref, mine_ref, other_ref) = refs[2 * chunks : 2 * chunks + 6], refs[2 * chunks + 6 :]

    @pl.when(pl.program_id(0) == 0)
    def _():
        for into, (own, near, far) in ((mine_ref, terms[:3]), (other_ref, terms[3:])):
            into[...] = (own[...] + near[...].astype(F32) + far[...].astype(F32)).astype(BF)

    for n in range(chunks):
        both = across(refs[n][...], mine_ref[...]) + across(refs[chunks + n][...], other_ref[...])
        share_ref[n] = both.astype(BF)


def project_kernel(*refs):
    parts, (weight_ref, out_ref) = refs[:-2], refs[-2:]
    width = parts[0].shape[1]
    out_ref[...] = sum(mm(part[...], weight_ref[n * width : (n + 1) * width, :]) for n, part in enumerate(parts))


def params(mib=56):
    return pltpu.CompilerParams(vmem_limit_bytes=mib * 1024 * 1024)


def picker(side, part):
    out = jnp.arange(128, dtype=jnp.int32)
    source = (out // part) * 2 * part + side * part + out % part
    return (jnp.arange(256, dtype=jnp.int32)[:, None] == source[None, :]).astype(BF)


def picked_columns(hidden, pick, chunk, chunks):
    rows, width = hidden.shape
    block = 1024
    steps = width // (block * chunks)
    return pl.pallas_call(
        pick_kernel,
        grid=(steps,),
        in_specs=[
            pl.BlockSpec((256, 128), lambda i: (0, 0)),
            pl.BlockSpec((rows, block), lambda i: (0, steps * chunk + i)),
        ],
        out_specs=pl.BlockSpec((rows, block // 2), lambda i: (0, i)),
        out_shape=jax.ShapeDtypeStruct((rows, steps * block // 2), BF),
        cost_estimate=pl.CostEstimate(flops=0, bytes_accessed=3 * rows * block * steps, transcendentals=0),
        compiler_params=params(),
        name="picked_columns",
    )(pick, hidden)


def chip_share(keep, came, terms):
    rows, width = keep.shape
    pair = terms[0].shape[1]
    chunks, steps = len(came), 2
    block = width // (steps * chunks)
    whole = pl.BlockSpec((rows, pair), lambda i: (0, 0))
    return pl.pallas_call(
        share_kernel,
        grid=(steps,),
        in_specs=[pl.BlockSpec((rows, block), lambda i, n=n: (0, steps * n + i)) for n in range(chunks)]
        + [pl.BlockSpec((rows, block), lambda i: (0, i))] * chunks
        + [whole] * len(terms),
        out_specs=pl.BlockSpec((chunks, block, pair), lambda i: (0, i, 0)),
        out_shape=jax.ShapeDtypeStruct((chunks, steps * block, pair), BF),
        scratch_shapes=[pltpu.VMEM((rows, pair), BF), pltpu.VMEM((rows, pair), BF)],
        cost_estimate=pl.CostEstimate(flops=4 * width * rows * pair, bytes_accessed=6 * width * rows, transcendentals=0),
        compiler_params=params(52),
        name="chip_share",
    )(*([keep] * chunks), *came, *terms)


def projected(came, weight):
    rows, pair = came[0].shape[0], weight.shape[1]
    return pl.pallas_call(
        project_kernel,
        out_shape=jax.ShapeDtypeStruct((rows, pair), F32),
        cost_estimate=pl.CostEstimate(flops=2 * rows * weight.size, bytes_accessed=2 * weight.size, transcendentals=0),
        compiler_params=params(16),
        name="projected",
    )(*came, weight)


def key_chunks(rows):
    edge, span = 2 * rows // 3, (SPAN + 1) * rows
    chunks = [(0, edge, 0, edge)]
    at = edge
    while at < span - edge:
        end = min(at + 768, span - edge)
        chunks.append((at, end, 0, rows))
        at = end
    chunks.append((span - edge, span, rows - edge, rows))
    return chunks


def onto_rows(total, extra, first, end):
    parts = [total[:first], total[first:end] + extra, total[end:]]
    return jnp.concatenate([part for part in parts if part.shape[0]], axis=0)


def lane_groups(block, size):
    return [block[:, n : n + size] for n in range(0, block.shape[1], size)]


def attention_kernel(place_ref, ends_ref, q_ref, g_ref, *refs):
    pieces = refs[:PIECES]
    out_ref, dq_ref, swap_ref, rest_ref, kv_ref, turned_ref, bias_ref, s_ref, p_ref, acc_ref = refs[PIECES:]
    step = pl.program_id(0)
    rows = q_ref.shape[0]
    size = kv_ref.shape[1] // 2
    span = kv_ref.shape[0]
    chunks = key_chunks(rows)
    scale = 1.0 / math.sqrt(size)
    scale2 = scale * math.log2(math.e)

    @pl.when(step == 0)
    def _():
        offset, core, ends = place_ref[0], place_ref[1], ends_ref[...]
        position = offset + lax.broadcasted_iota(jnp.int32, (rows, ends.shape[1]), 0)
        start = jnp.max(jnp.where(ends <= position, ends, 0), axis=1, keepdims=True)
        low = start - (offset - SPAN * rows)
        row = lax.broadcasted_iota(jnp.int32, (rows, rows), 0)
        own, second, fourth, other_own, other_second, other_fourth = [piece[...] for piece in pieces]
        first = jnp.where(core == 0, other_second, other_own)
        third = jnp.where(core == 0, other_fourth, other_second)
        for j, piece in enumerate([fourth, third, second, first, own]):
            cols = slice(j * rows, (j + 1) * rows)
            kv_ref[cols, :] = piece
            turned_ref[:size, cols] = piece[:, :size].T
            turned_ref[size:, cols] = piece[:, size:].T
            at = lax.broadcasted_iota(jnp.int32, (rows, rows), 1) + j * rows
            allowed = (at >= low) & (at <= row + SPAN * rows)
            bias_ref[:, cols] = jnp.where(allowed, 0.0, NEG)
        acc_ref[...] = jnp.zeros_like(acc_ref)

    def one_head(h):
        lanes = slice(h * size, (h + 1) * size)
        q = q_ref[:, lanes]
        top = jnp.full((rows, size), NEG, F32)
        for c0, c1, r0, r1 in chunks:
            s = mm(q[r0:r1], turned_ref[:size, c0:c1]) + bias_ref[r0:r1, c0:c1]
            s_ref[h % 2, r0:r1, c0:c1] = s
            most = functools.reduce(jnp.maximum, lane_groups(s, size))
            parts = [top[:r0], jnp.maximum(top[r0:r1], most), top[r1:]]
            top = jnp.concatenate([part for part in parts if part.shape[0]], axis=0)
            yield
        peak = jnp.max(top, axis=1, keepdims=True) * scale2
        total = jnp.zeros((rows, size), F32)
        out = jnp.zeros((rows, size), F32)
        for c0, c1, r0, r1 in chunks:
            e = jnp.exp2(s_ref[h % 2, r0:r1, c0:c1] * scale2 - peak[r0:r1])
            total = onto_rows(total, functools.reduce(jnp.add, lane_groups(e, size)), r0, r1)
            p = e.astype(BF)
            p_ref[h % 2, r0:r1, c0:c1] = p
            out = onto_rows(out, mm(p, kv_ref[c0:c1, size:]), r0, r1)
            yield
        inverse = 1.0 / jnp.sum(total, axis=1, keepdims=True)
        out = out * inverse
        out_ref[:, lanes] = out.astype(BF)
        scaled = g_ref[:, lanes].astype(F32) * inverse
        g = scaled.astype(BF)
        delta = jnp.sum(g.astype(F32) * out, axis=1, keepdims=True)
        g_turned = scaled.T.astype(BF)
        q_turned = q.astype(F32).T.astype(BF)
        dq = jnp.zeros((rows, size), F32)
        for c0, c1, r0, r1 in chunks:
            p = p_ref[h % 2, r0:r1, c0:c1]
            acc_ref[size:, c0:c1] += mm(g_turned[:, r0:r1], p)
            dp = mm(g[r0:r1], turned_ref[size:, c0:c1]) - delta[r0:r1]
            ds = dp.astype(BF) * p
            dq = onto_rows(dq, mm(ds, kv_ref[c0:c1, :size]), r0, r1)
            acc_ref[:size, c0:c1] += mm(q_turned[:, r0:r1], ds)
            yield
        dq_ref[:, lanes] = (dq * scale).astype(BF)

    running, waiting = [], [one_head(h) for h in range(q_ref.shape[1] // size)]
    while running or waiting:
        if waiting:
            running.append(waiting.pop(0))
        for _ in chunks:
            running = [head for head in running if next(head, head) is None]

    @pl.when(step == pl.num_programs(0) - 1)
    def _():
        for j in range(SPAN + 1):
            cols = slice(j * rows, (j + 1) * rows)
            into = rest_ref.at[j // 2] if j % 2 == 0 else swap_ref.at[1 - j // 2]
            into[:, :size] = (acc_ref[:size, cols].T * scale).astype(BF)
            into[:, size:] = acc_ref[size:, cols].T.astype(BF)


HEADS_PER_STEP = 8


def attention(place, ends, queries, out_grad, pieces):
    rows, width = queries.shape
    pair = pieces[0].shape[1]
    size = pair // 2
    heads = width // size
    span = (SPAN + 1) * rows
    several = pl.BlockSpec((rows, HEADS_PER_STEP * size), lambda h: (0, h))
    whole = pl.BlockSpec((rows, pair), lambda h: (0, 0))
    return pl.pallas_call(
        attention_kernel,
        grid=(heads // HEADS_PER_STEP,),
        in_specs=[
            pl.BlockSpec(memory_space=pltpu.SMEM),
            pl.BlockSpec((1, ends.shape[1]), lambda h: (0, 0)),
            several,
            several,
        ]
        + [whole] * PIECES,
        out_specs=[
            several,
            several,
            pl.BlockSpec((SPAN // 2, rows, pair), lambda h: (0, 0, 0)),
            pl.BlockSpec((SPAN // 2 + 1, rows, pair), lambda h: (0, 0, 0)),
        ],
        out_shape=[
            jax.ShapeDtypeStruct((rows, width), BF),
            jax.ShapeDtypeStruct((rows, width), BF),
            jax.ShapeDtypeStruct((SPAN // 2, rows, pair), BF),
            jax.ShapeDtypeStruct((SPAN // 2 + 1, rows, pair), BF),
        ],
        scratch_shapes=[
            pltpu.VMEM((span, pair), BF),
            pltpu.VMEM((pair, span), BF),
            pltpu.VMEM((rows, span), F32),
            pltpu.VMEM((2, rows, span), F32),
            pltpu.VMEM((2, rows, span), BF),
            pltpu.VMEM((pair, span), F32),
        ],
        cost_estimate=pl.CostEstimate(
            flops=24 * heads * rows * span * size, bytes_accessed=10 * rows * width, transcendentals=heads * rows * span
        ),
        compiler_params=params(56),
        name="attention",
    )(place, ends, queries, out_grad, *pieces)


def between_cores(block):
    return lax.ppermute(block, "core", SWAP)


def between_chips(block, distance):
    devices = range(lax.axis_size(ALL))
    route = [(i, i + 2 * distance) for i in devices if i + 2 * distance in devices]
    return lax.ppermute(block, ALL, route)


def window_pieces(key_value):
    second = between_chips(key_value, 1)
    fourth = between_chips(key_value, 2)
    mine = [key_value, second, fourth]
    return mine + [between_cores(block) for block in mine]


def returned(swap, rest, core):
    came = between_cores(swap)
    first, third = came[0].astype(F32), came[1].astype(F32)
    near = (rest[1].astype(F32) + jnp.where(core == 0, third, first)).astype(BF)
    far = (rest[0].astype(F32) + jnp.where(core == 0, 0.0, third)).astype(BF)
    own = rest[2].astype(F32) + jnp.where(core == 0, first, 0.0)
    terms = [own, between_chips(near, -1), between_chips(far, -2)]
    return terms + [between_cores(term) for term in terms]


def per_device(hidden, kv_weight, queries, out_grad, lengths):
    rows = hidden.shape[0]
    part, pair = kv_weight.shape
    core = lax.axis_index("core")
    chips = lax.axis_size(CHIPS)

    copies = jnp.broadcast_to(kv_weight[None], (chips, part, pair))
    weight = lax.all_to_all(copies, CHIPS, 0, 0, tiled=True).reshape(chips * part, pair)

    away = picker(1 - core, part)
    came = [between_cores(picked_columns(hidden, away, n, CHUNKS)) for n in range(CHUNKS)]
    keep = picked_columns(hidden, picker(core, part), 0, 1)

    place = jnp.stack([lax.axis_index(ALL) * rows, core]).astype(jnp.int32)
    ends = jnp.cumsum(lengths).astype(jnp.int32)[None, :]

    place, ends, keep = lax.optimization_barrier((place, ends, keep))
    partner = between_cores(projected(came, weight))
    key_value = (mm(keep, weight) + partner).astype(BF)
    pieces = window_pieces(key_value)

    attended, query_grad, swap, rest = attention(place, ends, queries, out_grad, pieces)
    share = chip_share(keep, came, returned(swap, rest, core)).reshape(chips, part, pair)
    spread = lax.all_to_all(share, CHIPS, 0, 0, tiled=True)
    return attended, query_grad, jnp.sum(spread.astype(F32), axis=0)


def solution(mesh):
    cuts, dp = mesh.devices.shape
    fine = Mesh(mesh.devices.reshape(cuts, 4, dp // 8, 2), ALL)
    rows = P(ALL, None)
    return jax.shard_map(
        per_device,
        mesh=fine,
        in_specs=(rows, rows, rows, rows, P()),
        out_specs=(rows, rows, rows),
        check_vma=False,
    )
```

```python
import functools
import math

import jax
import jax.numpy as jnp
from jax import lax
from jax.experimental import pallas as pl
from jax.experimental.pallas import tpu as pltpu
from jax.sharding import Mesh, PartitionSpec as P

SPAN = 4
PIECES = 6
NEG = -1e30
CHIPS = ("z", "x", "y")
ALL = ("z", "x", "y", "core")
SWAP = [(0, 1), (1, 0)]
CHUNKS = 4
BF = jnp.bfloat16
F32 = jnp.float32


def mm(a, b):
    return jnp.dot(a, b, preferred_element_type=F32)


def pick_kernel(pick_ref, x_ref, out_ref):
    for n in range(x_ref.shape[1] // 256):
        y = mm(x_ref[:, n * 256 : (n + 1) * 256], pick_ref[...])
        out_ref[:, n * 128 : (n + 1) * 128] = y.astype(BF)


def across(a, b):
    return lax.dot_general(a, b, (((0,), (0,)), ((), ())), preferred_element_type=F32)


def share_kernel(*refs):
    chunks = (len(refs) - 9) // 2
    terms, (share_ref, mine_ref, other_ref) = refs[2 * chunks : 2 * chunks + 6], refs[2 * chunks + 6 :]

    @pl.when(pl.program_id(0) == 0)
    def _():
        for into, (own, near, far) in ((mine_ref, terms[:3]), (other_ref, terms[3:])):
            into[...] = (own[...] + near[...].astype(F32) + far[...].astype(F32)).astype(BF)

    for n in range(chunks):
        both = across(refs[n][...], mine_ref[...]) + across(refs[chunks + n][...], other_ref[...])
        share_ref[n] = both.astype(BF)


def project_kernel(*refs):
    parts, (weight_ref, out_ref) = refs[:-2], refs[-2:]
    width = parts[0].shape[1]
    out_ref[...] = sum(mm(part[...], weight_ref[n * width : (n + 1) * width, :]) for n, part in enumerate(parts))


def params(mib=56):
    return pltpu.CompilerParams(vmem_limit_bytes=mib * 1024 * 1024)


def picker(side, part):
    out = jnp.arange(128, dtype=jnp.int32)
    source = (out // part) * 2 * part + side * part + out % part
    return (jnp.arange(256, dtype=jnp.int32)[:, None] == source[None, :]).astype(BF)


def picked_columns(hidden, pick, chunk, chunks):
    rows, width = hidden.shape
    block = 1024
    steps = width // (block * chunks)
    return pl.pallas_call(
        pick_kernel,
        grid=(steps,),
        in_specs=[
            pl.BlockSpec((256, 128), lambda i: (0, 0)),
            pl.BlockSpec((rows, block), lambda i: (0, steps * chunk + i)),
        ],
        out_specs=pl.BlockSpec((rows, block // 2), lambda i: (0, i)),
        out_shape=jax.ShapeDtypeStruct((rows, steps * block // 2), BF),
        cost_estimate=pl.CostEstimate(flops=0, bytes_accessed=3 * rows * block * steps, transcendentals=0),
        compiler_params=params(),
        name="picked_columns",
    )(pick, hidden)


def chip_share(keep, came, terms):
    rows, width = keep.shape
    pair = terms[0].shape[1]
    chunks, steps = len(came), 2
    block = width // (steps * chunks)
    whole = pl.BlockSpec((rows, pair), lambda i: (0, 0))
    return pl.pallas_call(
        share_kernel,
        grid=(steps,),
        in_specs=[pl.BlockSpec((rows, block), lambda i, n=n: (0, steps * n + i)) for n in range(chunks)]
        + [pl.BlockSpec((rows, block), lambda i: (0, i))] * chunks
        + [whole] * len(terms),
        out_specs=pl.BlockSpec((chunks, block, pair), lambda i: (0, i, 0)),
        out_shape=jax.ShapeDtypeStruct((chunks, steps * block, pair), BF),
        scratch_shapes=[pltpu.VMEM((rows, pair), BF), pltpu.VMEM((rows, pair), BF)],
        cost_estimate=pl.CostEstimate(flops=4 * width * rows * pair, bytes_accessed=6 * width * rows, transcendentals=0),
        compiler_params=params(52),
        name="chip_share",
    )(*([keep] * chunks), *came, *terms)


def projected(came, weight):
    rows, pair = came[0].shape[0], weight.shape[1]
    return pl.pallas_call(
        project_kernel,
        out_shape=jax.ShapeDtypeStruct((rows, pair), F32),
        cost_estimate=pl.CostEstimate(flops=2 * rows * weight.size, bytes_accessed=2 * weight.size, transcendentals=0),
        compiler_params=params(16),
        name="projected",
    )(*came, weight)


def key_chunks(rows):
    edge, span = 2 * rows // 3, (SPAN + 1) * rows
    chunks = [(0, edge, 0, edge)]
    at = edge
    while at < span - edge:
        end = min(at + 768, span - edge)
        chunks.append((at, end, 0, rows))
        at = end
    chunks.append((span - edge, span, rows - edge, rows))
    return chunks


def onto_rows(total, extra, first, end):
    parts = [total[:first], total[first:end] + extra, total[end:]]
    return jnp.concatenate([part for part in parts if part.shape[0]], axis=0)


def lane_groups(block, size):
    return [block[:, n : n + size] for n in range(0, block.shape[1], size)]


def attention_kernel(place_ref, ends_ref, q_hbm, g_hbm, *refs):
    pieces = refs[:PIECES]
    out_hbm, dq_hbm, swap_ref, rest_ref, kv_ref, turned_ref, bias_ref, s_ref, p_ref, acc_ref, *refs = refs[PIECES:]
    q_ref, g_ref, out_ref, dq_ref, sems = refs
    rows = q_ref.shape[0]
    size = kv_ref.shape[1] // 2
    span = kv_ref.shape[0]
    heads = q_ref.shape[1] // size

    arriving = [pltpu.make_async_copy(q_hbm, q_ref, sems.at[0]), pltpu.make_async_copy(g_hbm, g_ref, sems.at[1])]
    leaving = [pltpu.make_async_copy(out_ref, out_hbm, sems.at[2]), pltpu.make_async_copy(dq_ref, dq_hbm, sems.at[3])]
    for copy in arriving:
        copy.start()
    chunks = key_chunks(rows)
    scale = 1.0 / math.sqrt(size)
    scale2 = scale * math.log2(math.e)

    offset, core, ends = place_ref[0], place_ref[1], ends_ref[...]
    position = offset + lax.broadcasted_iota(jnp.int32, (rows, ends.shape[1]), 0)
    start = jnp.max(jnp.where(ends <= position, ends, 0), axis=1, keepdims=True)
    low = start - (offset - SPAN * rows)
    row = lax.broadcasted_iota(jnp.int32, (rows, rows), 0)
    own, second, fourth, other_own, other_second, other_fourth = [piece[...] for piece in pieces]
    first = jnp.where(core == 0, other_second, other_own)
    third = jnp.where(core == 0, other_fourth, other_second)
    for j, piece in enumerate([fourth, third, second, first, own]):
        cols = slice(j * rows, (j + 1) * rows)
        kv_ref[cols, :] = piece
        turned_ref[:size, cols] = piece[:, :size].T
        turned_ref[size:, cols] = piece[:, size:].T
        at = lax.broadcasted_iota(jnp.int32, (rows, rows), 1) + j * rows
        allowed = (at >= low) & (at <= row + SPAN * rows)
        bias_ref[:, cols] = jnp.where(allowed, 0.0, NEG)
    acc_ref[...] = jnp.zeros_like(acc_ref)
    for copy in arriving:
        copy.wait()

    def one_head(h):
        lanes = slice(h * size, (h + 1) * size)
        q = q_ref[:, lanes]
        top = jnp.full((rows, size), NEG, F32)
        for c0, c1, r0, r1 in chunks:
            s = mm(q[r0:r1], turned_ref[:size, c0:c1]) + bias_ref[r0:r1, c0:c1]
            s_ref[h % 2, r0:r1, c0:c1] = s
            most = functools.reduce(jnp.maximum, lane_groups(s, size))
            parts = [top[:r0], jnp.maximum(top[r0:r1], most), top[r1:]]
            top = jnp.concatenate([part for part in parts if part.shape[0]], axis=0)
            yield
        peak = jnp.max(top, axis=1, keepdims=True) * scale2
        total = jnp.zeros((rows, size), F32)
        out = jnp.zeros((rows, size), F32)
        for c0, c1, r0, r1 in chunks:
            e = jnp.exp2(s_ref[h % 2, r0:r1, c0:c1] * scale2 - peak[r0:r1])
            total = onto_rows(total, functools.reduce(jnp.add, lane_groups(e, size)), r0, r1)
            p = e.astype(BF)
            p_ref[h % 2, r0:r1, c0:c1] = p
            out = onto_rows(out, mm(p, kv_ref[c0:c1, size:]), r0, r1)
            yield
        inverse = 1.0 / jnp.sum(total, axis=1, keepdims=True)
        out = out * inverse
        out_ref[:, lanes] = out.astype(BF)
        scaled = g_ref[:, lanes].astype(F32) * inverse
        g = scaled.astype(BF)
        delta = jnp.sum(g.astype(F32) * out, axis=1, keepdims=True)
        g_turned = scaled.T.astype(BF)
        q_turned = q.astype(F32).T.astype(BF)
        dq = jnp.zeros((rows, size), F32)
        for c0, c1, r0, r1 in chunks:
            p = p_ref[h % 2, r0:r1, c0:c1]
            acc_ref[size:, c0:c1] += mm(g_turned[:, r0:r1], p)
            dp = mm(g[r0:r1], turned_ref[size:, c0:c1]) - delta[r0:r1]
            ds = dp.astype(BF) * p
            dq = onto_rows(dq, mm(ds, kv_ref[c0:c1, :size]), r0, r1)
            acc_ref[:size, c0:c1] += mm(q_turned[:, r0:r1], ds)
            yield
        dq_ref[:, lanes] = (dq * scale).astype(BF)

    running, waiting = [], [one_head(h) for h in range(heads)]
    while running or waiting:
        if waiting:
            running.append(waiting.pop(0))
        for _ in chunks:
            running = [head for head in running if next(head, head) is None]

    for copy in leaving:
        copy.start()
    for j in range(SPAN + 1):
        cols = slice(j * rows, (j + 1) * rows)
        into = rest_ref.at[j // 2] if j % 2 == 0 else swap_ref.at[1 - j // 2]
        into[:, :size] = (acc_ref[:size, cols].T * scale).astype(BF)
        into[:, size:] = acc_ref[size:, cols].T.astype(BF)
    for copy in leaving:
        copy.wait()


def attention(place, ends, queries, out_grad, pieces):
    rows, width = queries.shape
    pair = pieces[0].shape[1]
    size = pair // 2
    heads = width // size
    span = (SPAN + 1) * rows
    far_off = pl.BlockSpec(memory_space=pltpu.HBM)
    near_by = pl.BlockSpec(memory_space=pltpu.VMEM)
    return pl.pallas_call(
        attention_kernel,
        in_specs=[pl.BlockSpec(memory_space=pltpu.SMEM), near_by, far_off, far_off] + [near_by] * PIECES,
        out_specs=[far_off, far_off, near_by, near_by],
        out_shape=[
            jax.ShapeDtypeStruct((rows, width), BF),
            jax.ShapeDtypeStruct((rows, width), BF),
            jax.ShapeDtypeStruct((SPAN // 2, rows, pair), BF),
            jax.ShapeDtypeStruct((SPAN // 2 + 1, rows, pair), BF),
        ],
        scratch_shapes=[
            pltpu.VMEM((span, pair), BF),
            pltpu.VMEM((pair, span), BF),
            pltpu.VMEM((rows, span), F32),
            pltpu.VMEM((2, rows, span), F32),
            pltpu.VMEM((2, rows, span), BF),
            pltpu.VMEM((pair, span), F32),
            pltpu.VMEM((rows, width), BF),
            pltpu.VMEM((rows, width), BF),
            pltpu.VMEM((rows, width), BF),
            pltpu.VMEM((rows, width), BF),
            pltpu.SemaphoreType.DMA((4,)),
        ],
        cost_estimate=pl.CostEstimate(
            flops=24 * heads * rows * span * size, bytes_accessed=10 * rows * width, transcendentals=heads * rows * span
        ),
        compiler_params=params(36),
        name="attention",
    )(place, ends, queries, out_grad, *pieces)


def between_cores(block):
    return lax.ppermute(block, "core", SWAP)


def between_chips(block, distance):
    devices = range(lax.axis_size(ALL))
    route = [(i, i + 2 * distance) for i in devices if i + 2 * distance in devices]
    return lax.ppermute(block, ALL, route)


def window_pieces(key_value):
    second = between_chips(key_value, 1)
    fourth = between_chips(key_value, 2)
    mine = [key_value, second, fourth]
    return mine + [between_cores(block) for block in mine]


def returned(swap, rest, core):
    came = between_cores(swap)
    first, third = came[0].astype(F32), came[1].astype(F32)
    near = (rest[1].astype(F32) + jnp.where(core == 0, third, first)).astype(BF)
    far = (rest[0].astype(F32) + jnp.where(core == 0, 0.0, third)).astype(BF)
    own = rest[2].astype(F32) + jnp.where(core == 0, first, 0.0)
    terms = [own, between_chips(near, -1), between_chips(far, -2)]
    return terms + [between_cores(term) for term in terms]


def per_device(hidden, kv_weight, queries, out_grad, lengths):
    rows = hidden.shape[0]
    part, pair = kv_weight.shape
    core = lax.axis_index("core")
    chips = lax.axis_size(CHIPS)

    copies = jnp.broadcast_to(kv_weight[None], (chips, part, pair))
    weight = lax.all_to_all(copies, CHIPS, 0, 0, tiled=True).reshape(chips * part, pair)

    away = picker(1 - core, part)
    came = [between_cores(picked_columns(hidden, away, n, CHUNKS)) for n in range(CHUNKS)]
    keep = picked_columns(hidden, picker(core, part), 0, 1)

    place = jnp.stack([lax.axis_index(ALL) * rows, core]).astype(jnp.int32)
    ends = jnp.cumsum(lengths).astype(jnp.int32)[None, :]

    place, ends, keep = lax.optimization_barrier((place, ends, keep))
    partner = between_cores(projected(came, weight))
    key_value = (mm(keep, weight) + partner).astype(BF)
    pieces = window_pieces(key_value)

    attended, query_grad, swap, rest = attention(place, ends, queries, out_grad, pieces)
    share = chip_share(keep, came, returned(swap, rest, core)).reshape(chips, part, pair)
    spread = lax.all_to_all(share, CHIPS, 0, 0, tiled=True)
    return attended, query_grad, jnp.sum(spread.astype(F32), axis=0)


def solution(mesh):
    cuts, dp = mesh.devices.shape
    fine = Mesh(mesh.devices.reshape(cuts, 4, dp // 8, 2), ALL)
    rows = P(ALL, None)
    return jax.shard_map(
        per_device,
        mesh=fine,
        in_specs=(rows, rows, rows, rows, P()),
        out_specs=(rows, rows, rows),
        check_vma=False,
    )
```

```python
import functools
import math

import jax
import jax.numpy as jnp
from jax import lax
from jax.experimental import pallas as pl
from jax.experimental.pallas import tpu as pltpu
from jax.sharding import Mesh, PartitionSpec as P

SPAN = 4
PIECES = 6
NEG = -1e30
CHIPS = ("z", "x", "y")
ALL = ("z", "x", "y", "core")
SWAP = [(0, 1), (1, 0)]
CHUNKS = 4
BF = jnp.bfloat16
F32 = jnp.float32


def mm(a, b):
    return jnp.dot(a, b, preferred_element_type=F32)


def pick_kernel(pick_ref, x_ref, out_ref):
    for n in range(x_ref.shape[1] // 256):
        y = mm(x_ref[:, n * 256 : (n + 1) * 256], pick_ref[...])
        out_ref[:, n * 128 : (n + 1) * 128] = y.astype(BF)


def across(a, b):
    return lax.dot_general(a, b, (((0,), (0,)), ((), ())), preferred_element_type=F32)


def share_kernel(*refs):
    chunks = (len(refs) - 9) // 2
    terms, (share_ref, mine_ref, other_ref) = refs[2 * chunks : 2 * chunks + 6], refs[2 * chunks + 6 :]

    @pl.when(pl.program_id(0) == 0)
    def _():
        for into, (own, near, far) in ((mine_ref, terms[:3]), (other_ref, terms[3:])):
            into[...] = (own[...] + near[...].astype(F32) + far[...].astype(F32)).astype(BF)

    for n in range(chunks):
        both = across(refs[n][...], mine_ref[...]) + across(refs[chunks + n][...], other_ref[...])
        share_ref[n] = both.astype(BF)


def project_kernel(*refs):
    parts, (weight_ref, out_ref) = refs[:-2], refs[-2:]
    width = parts[0].shape[1]
    out_ref[...] = sum(mm(part[...], weight_ref[n * width : (n + 1) * width, :]) for n, part in enumerate(parts))


def params(mib=56):
    return pltpu.CompilerParams(vmem_limit_bytes=mib * 1024 * 1024)


def picker(side, part):
    out = jnp.arange(128, dtype=jnp.int32)
    source = (out // part) * 2 * part + side * part + out % part
    return (jnp.arange(256, dtype=jnp.int32)[:, None] == source[None, :]).astype(BF)


def picked_columns(hidden, pick, chunk, chunks):
    rows, width = hidden.shape
    block = 1024
    steps = width // (block * chunks)
    return pl.pallas_call(
        pick_kernel,
        grid=(steps,),
        in_specs=[
            pl.BlockSpec((256, 128), lambda i: (0, 0)),
            pl.BlockSpec((rows, block), lambda i: (0, steps * chunk + i)),
        ],
        out_specs=pl.BlockSpec((rows, block // 2), lambda i: (0, i)),
        out_shape=jax.ShapeDtypeStruct((rows, steps * block // 2), BF),
        cost_estimate=pl.CostEstimate(flops=0, bytes_accessed=3 * rows * block * steps, transcendentals=0),
        compiler_params=params(),
        name="picked_columns",
    )(pick, hidden)


def chip_share(keep, came, terms):
    rows, width = keep.shape
    pair = terms[0].shape[1]
    chunks, steps = len(came), 2
    block = width // (steps * chunks)
    whole = pl.BlockSpec((rows, pair), lambda i: (0, 0))
    return pl.pallas_call(
        share_kernel,
        grid=(steps,),
        in_specs=[pl.BlockSpec((rows, block), lambda i, n=n: (0, steps * n + i)) for n in range(chunks)]
        + [pl.BlockSpec((rows, block), lambda i: (0, i))] * chunks
        + [whole] * len(terms),
        out_specs=pl.BlockSpec((chunks, block, pair), lambda i: (0, i, 0)),
        out_shape=jax.ShapeDtypeStruct((chunks, steps * block, pair), BF),
        scratch_shapes=[pltpu.VMEM((rows, pair), BF), pltpu.VMEM((rows, pair), BF)],
        cost_estimate=pl.CostEstimate(flops=4 * width * rows * pair, bytes_accessed=6 * width * rows, transcendentals=0),
        compiler_params=params(47),
        name="chip_share",
    )(*([keep] * chunks), *came, *terms)


def projected(came, weight):
    rows, pair = came[0].shape[0], weight.shape[1]
    return pl.pallas_call(
        project_kernel,
        out_shape=jax.ShapeDtypeStruct((rows, pair), F32),
        cost_estimate=pl.CostEstimate(flops=2 * rows * weight.size, bytes_accessed=2 * weight.size, transcendentals=0),
        compiler_params=params(16),
        name="projected",
    )(*came, weight)


def key_chunks(rows):
    edge, span = 2 * rows // 3, (SPAN + 1) * rows
    chunks = [(0, edge, 0, edge)]
    at = edge
    while at < span - edge:
        end = min(at + 1024, span - edge)
        chunks.append((at, end, 0, rows))
        at = end
    chunks.append((span - edge, span, rows - edge, rows))
    return chunks


def onto_rows(total, extra, first, end):
    parts = [total[:first], total[first:end] + extra, total[end:]]
    return jnp.concatenate([part for part in parts if part.shape[0]], axis=0)


def lane_groups(block, size):
    return [block[:, n : n + size] for n in range(0, block.shape[1], size)]


def attention_kernel(place_ref, ends_ref, q_hbm, g_hbm, *refs):
    pieces = refs[:PIECES]
    out_hbm, dq_hbm, swap_ref, rest_ref, kv_ref, turned_ref, bias_ref, s_ref, p_ref, acc_ref, *refs = refs[PIECES:]
    q_ref, g_ref, out_ref, dq_ref, sems = refs
    rows = q_ref.shape[0]
    size = kv_ref.shape[1] // 2
    span = kv_ref.shape[0]
    heads = q_ref.shape[1] // size

    arriving = [pltpu.make_async_copy(q_hbm, q_ref, sems.at[0]), pltpu.make_async_copy(g_hbm, g_ref, sems.at[1])]
    leaving = [pltpu.make_async_copy(out_ref, out_hbm, sems.at[2]), pltpu.make_async_copy(dq_ref, dq_hbm, sems.at[3])]
    for copy in arriving:
        copy.start()
    chunks = key_chunks(rows)
    scale = 1.0 / math.sqrt(size)
    scale2 = scale * math.log2(math.e)

    offset, core, ends = place_ref[0], place_ref[1], ends_ref[...]
    position = offset + lax.broadcasted_iota(jnp.int32, (rows, ends.shape[1]), 0)
    start = jnp.max(jnp.where(ends <= position, ends, 0), axis=1, keepdims=True)
    low = start - (offset - SPAN * rows)
    row = lax.broadcasted_iota(jnp.int32, (rows, rows), 0)
    own, second, fourth, other_own, other_second, other_fourth = [piece[...] for piece in pieces]
    first = jnp.where(core == 0, other_second, other_own)
    third = jnp.where(core == 0, other_fourth, other_second)
    for j, piece in enumerate([fourth, third, second, first, own]):
        cols = slice(j * rows, (j + 1) * rows)
        kv_ref[cols, :] = piece
        turned_ref[:size, cols] = piece[:, :size].T
        turned_ref[size:, cols] = piece[:, size:].T
        at = lax.broadcasted_iota(jnp.int32, (rows, rows), 1) + j * rows
        allowed = (at >= low) & (at <= row + SPAN * rows)
        bias_ref[:, cols] = jnp.where(allowed, 0.0, NEG)
    acc_ref[...] = jnp.zeros_like(acc_ref)
    for copy in arriving:
        copy.wait()

    def one_head(h):
        lanes = slice(h * size, (h + 1) * size)
        q = q_ref[:, lanes]
        top = jnp.full((rows, size), NEG, F32)
        for c0, c1, r0, r1 in chunks:
            s = mm(q[r0:r1], turned_ref[:size, c0:c1]) + bias_ref[r0:r1, c0:c1]
            s_ref[h % 2, r0:r1, c0:c1] = s
            most = functools.reduce(jnp.maximum, lane_groups(s, size))
            parts = [top[:r0], jnp.maximum(top[r0:r1], most), top[r1:]]
            top = jnp.concatenate([part for part in parts if part.shape[0]], axis=0)
            yield
        peak = jnp.max(top, axis=1, keepdims=True) * scale2
        total = jnp.zeros((rows, size), F32)
        out = jnp.zeros((rows, size), F32)
        for c0, c1, r0, r1 in chunks:
            e = jnp.exp2(s_ref[h % 2, r0:r1, c0:c1] * scale2 - peak[r0:r1])
            total = onto_rows(total, functools.reduce(jnp.add, lane_groups(e, size)), r0, r1)
            p = e.astype(BF)
            p_ref[h % 2, r0:r1, c0:c1] = p
            out = onto_rows(out, mm(p, kv_ref[c0:c1, size:]), r0, r1)
            yield
        inverse = 1.0 / jnp.sum(total, axis=1, keepdims=True)
        out = out * inverse
        out_ref[:, lanes] = out.astype(BF)
        scaled = g_ref[:, lanes].astype(F32) * inverse
        g = scaled.astype(BF)
        delta = jnp.sum(g.astype(F32) * out, axis=1, keepdims=True)
        g_turned = scaled.T.astype(BF)
        q_turned = q.astype(F32).T.astype(BF)
        dq = jnp.zeros((rows, size), F32)
        for c0, c1, r0, r1 in chunks:
            p = p_ref[h % 2, r0:r1, c0:c1]
            acc_ref[size:, c0:c1] += mm(g_turned[:, r0:r1], p)
            dp = mm(g[r0:r1], turned_ref[size:, c0:c1]) - delta[r0:r1]
            ds = dp.astype(BF) * p
            dq = onto_rows(dq, mm(ds, kv_ref[c0:c1, :size]), r0, r1)
            acc_ref[:size, c0:c1] += mm(q_turned[:, r0:r1], ds)
            yield
        dq_ref[:, lanes] = (dq * scale).astype(BF)

    running, waiting = [], [one_head(h) for h in range(heads)]
    while running or waiting:
        if waiting:
            running.append(waiting.pop(0))
        for _ in chunks:
            running = [head for head in running if next(head, head) is None]

    for copy in leaving:
        copy.start()
    for j in range(SPAN + 1):
        cols = slice(j * rows, (j + 1) * rows)
        into = rest_ref.at[j // 2] if j % 2 == 0 else swap_ref.at[1 - j // 2]
        into[:, :size] = (acc_ref[:size, cols].T * scale).astype(BF)
        into[:, size:] = acc_ref[size:, cols].T.astype(BF)
    for copy in leaving:
        copy.wait()


def attention(place, ends, queries, out_grad, pieces):
    rows, width = queries.shape
    pair = pieces[0].shape[1]
    size = pair // 2
    heads = width // size
    span = (SPAN + 1) * rows
    far_off = pl.BlockSpec(memory_space=pltpu.HBM)
    near_by = pl.BlockSpec(memory_space=pltpu.VMEM)
    return pl.pallas_call(
        attention_kernel,
        in_specs=[pl.BlockSpec(memory_space=pltpu.SMEM), near_by, far_off, far_off] + [near_by] * PIECES,
        out_specs=[far_off, far_off, near_by, near_by],
        out_shape=[
            jax.ShapeDtypeStruct((rows, width), BF),
            jax.ShapeDtypeStruct((rows, width), BF),
            jax.ShapeDtypeStruct((SPAN // 2, rows, pair), BF),
            jax.ShapeDtypeStruct((SPAN // 2 + 1, rows, pair), BF),
        ],
        scratch_shapes=[
            pltpu.VMEM((span, pair), BF),
            pltpu.VMEM((pair, span), BF),
            pltpu.VMEM((rows, span), F32),
            pltpu.VMEM((2, rows, span), F32),
            pltpu.VMEM((2, rows, span), BF),
            pltpu.VMEM((pair, span), F32),
            pltpu.VMEM((rows, width), BF),
            pltpu.VMEM((rows, width), BF),
            pltpu.VMEM((rows, width), BF),
            pltpu.VMEM((rows, width), BF),
            pltpu.SemaphoreType.DMA((4,)),
        ],
        cost_estimate=pl.CostEstimate(
            flops=24 * heads * rows * span * size, bytes_accessed=10 * rows * width, transcendentals=heads * rows * span
        ),
        compiler_params=params(36),
        name="attention",
    )(place, ends, queries, out_grad, *pieces)


def between_cores(block):
    return lax.ppermute(block, "core", SWAP)


def between_chips(block, distance):
    devices = range(lax.axis_size(ALL))
    route = [(i, i + 2 * distance) for i in devices if i + 2 * distance in devices]
    return lax.ppermute(block, ALL, route)


def window_pieces(key_value):
    second = between_chips(key_value, 1)
    fourth = between_chips(key_value, 2)
    mine = [key_value, second, fourth]
    return mine + [between_cores(block) for block in mine]


def returned(swap, rest, core):
    came = between_cores(swap)
    first, third = came[0].astype(F32), came[1].astype(F32)
    near = (rest[1].astype(F32) + jnp.where(core == 0, third, first)).astype(BF)
    far = (rest[0].astype(F32) + jnp.where(core == 0, 0.0, third)).astype(BF)
    own = rest[2].astype(F32) + jnp.where(core == 0, first, 0.0)
    terms = [own, between_chips(near, -1), between_chips(far, -2)]
    return terms + [between_cores(term) for term in terms]


def per_device(hidden, kv_weight, queries, out_grad, lengths):
    rows = hidden.shape[0]
    part, pair = kv_weight.shape
    core = lax.axis_index("core")
    chips = lax.axis_size(CHIPS)

    copies = jnp.broadcast_to(kv_weight[None], (chips, part, pair))
    weight = lax.all_to_all(copies, CHIPS, 0, 0, tiled=True).reshape(chips * part, pair)

    away = picker(1 - core, part)
    came = [between_cores(picked_columns(hidden, away, n, CHUNKS)) for n in range(CHUNKS)]
    keep = picked_columns(hidden, picker(core, part), 0, 1)

    place = jnp.stack([lax.axis_index(ALL) * rows, core]).astype(jnp.int32)
    ends = jnp.cumsum(lengths).astype(jnp.int32)[None, :]

    place, ends, keep = lax.optimization_barrier((place, ends, keep))
    partner = between_cores(projected(came, weight))
    key_value = (mm(keep, weight) + partner).astype(BF)
    pieces = window_pieces(key_value)

    attended, query_grad, swap, rest = attention(place, ends, queries, out_grad, pieces)
    share = chip_share(keep, came, returned(swap, rest, core)).reshape(chips, part, pair)
    spread = lax.all_to_all(share, CHIPS, 0, 0, tiled=True)
    return attended, query_grad, jnp.sum(spread.astype(F32), axis=0)


def solution(mesh):
    cuts, dp = mesh.devices.shape
    fine = Mesh(mesh.devices.reshape(cuts, 4, dp // 8, 2), ALL)
    rows = P(ALL, None)
    return jax.shard_map(
        per_device,
        mesh=fine,
        in_specs=(rows, rows, rows, rows, P()),
        out_specs=(rows, rows, rows),
        check_vma=False,
    )
```

```python
import functools
import math

import jax
import jax.numpy as jnp
from jax import lax
from jax.experimental import pallas as pl
from jax.experimental.pallas import tpu as pltpu
from jax.sharding import Mesh, PartitionSpec as P

SPAN = 4
PIECES = 6
NEG = -1e30
CHIPS = ("z", "x", "y")
ALL = ("z", "x", "y", "core")
SWAP = [(0, 1), (1, 0)]
CHUNKS = 4
BF = jnp.bfloat16
F32 = jnp.float32


def mm(a, b):
    return jnp.dot(a, b, preferred_element_type=F32)


def pick_kernel(pick_ref, x_ref, out_ref):
    for n in range(x_ref.shape[1] // 256):
        y = mm(x_ref[:, n * 256 : (n + 1) * 256], pick_ref[...])
        out_ref[:, n * 128 : (n + 1) * 128] = y.astype(BF)


def across(a, b):
    return lax.dot_general(a, b, (((0,), (0,)), ((), ())), preferred_element_type=F32)


def share_kernel(*refs):
    chunks = (len(refs) - 9) // 2
    terms, (share_ref, mine_ref, other_ref) = refs[2 * chunks : 2 * chunks + 6], refs[2 * chunks + 6 :]

    @pl.when(pl.program_id(0) == 0)
    def _():
        for into, (own, near, far) in ((mine_ref, terms[:3]), (other_ref, terms[3:])):
            into[...] = (own[...] + near[...].astype(F32) + far[...].astype(F32)).astype(BF)

    for n in range(chunks):
        both = across(refs[n][...], mine_ref[...]) + across(refs[chunks + n][...], other_ref[...])
        share_ref[n] = both.astype(BF)


def project_kernel(*refs):
    parts, (weight_ref, out_ref) = refs[:-2], refs[-2:]
    width = parts[0].shape[1]
    out_ref[...] = sum(mm(part[...], weight_ref[n * width : (n + 1) * width, :]) for n, part in enumerate(parts))


def params(mib=56):
    return pltpu.CompilerParams(vmem_limit_bytes=mib * 1024 * 1024)


def picker(side, part):
    out = jnp.arange(128, dtype=jnp.int32)
    source = (out // part) * 2 * part + side * part + out % part
    return (jnp.arange(256, dtype=jnp.int32)[:, None] == source[None, :]).astype(BF)


def picked_columns(hidden, pick, chunk, chunks):
    rows, width = hidden.shape
    block = 1024
    steps = width // (block * chunks)
    return pl.pallas_call(
        pick_kernel,
        grid=(steps,),
        in_specs=[
            pl.BlockSpec((256, 128), lambda i: (0, 0)),
            pl.BlockSpec((rows, block), lambda i: (0, steps * chunk + i)),
        ],
        out_specs=pl.BlockSpec((rows, block // 2), lambda i: (0, i)),
        out_shape=jax.ShapeDtypeStruct((rows, steps * block // 2), BF),
        cost_estimate=pl.CostEstimate(flops=0, bytes_accessed=3 * rows * block * steps, transcendentals=0),
        compiler_params=params(),
        name="picked_columns",
    )(pick, hidden)


def chip_share(keep, came, terms):
    rows, width = keep.shape
    pair = terms[0].shape[1]
    chunks, steps = len(came), 2
    block = width // (steps * chunks)
    whole = pl.BlockSpec((rows, pair), lambda i: (0, 0))
    return pl.pallas_call(
        share_kernel,
        grid=(steps,),
        in_specs=[pl.BlockSpec((rows, block), lambda i, n=n: (0, steps * n + i)) for n in range(chunks)]
        + [pl.BlockSpec((rows, block), lambda i: (0, i))] * chunks
        + [whole] * len(terms),
        out_specs=pl.BlockSpec((chunks, block, pair), lambda i: (0, i, 0)),
        out_shape=jax.ShapeDtypeStruct((chunks, steps * block, pair), BF),
        scratch_shapes=[pltpu.VMEM((rows, pair), BF), pltpu.VMEM((rows, pair), BF)],
        cost_estimate=pl.CostEstimate(flops=4 * width * rows * pair, bytes_accessed=6 * width * rows, transcendentals=0),
        compiler_params=params(47),
        name="chip_share",
    )(*([keep] * chunks), *came, *terms)


def projected(came, weight):
    rows, pair = came[0].shape[0], weight.shape[1]
    return pl.pallas_call(
        project_kernel,
        out_shape=jax.ShapeDtypeStruct((rows, pair), F32),
        cost_estimate=pl.CostEstimate(flops=2 * rows * weight.size, bytes_accessed=2 * weight.size, transcendentals=0),
        compiler_params=params(16),
        name="projected",
    )(*came, weight)


def key_chunks(rows):
    edge, span = 2 * rows // 3, (SPAN + 1) * rows
    chunks = [(0, edge, 0, edge)]
    at = edge
    while at < span - edge:
        end = min(at + 1024, span - edge)
        chunks.append((at, end, 0, rows))
        at = end
    chunks.append((span - edge, span, rows - edge, rows))
    return chunks


def onto_rows(total, extra, first, end):
    parts = [total[:first], total[first:end] + extra, total[end:]]
    return jnp.concatenate([part for part in parts if part.shape[0]], axis=0)


def lane_groups(block, size):
    return [block[:, n : n + size] for n in range(0, block.shape[1], size)]


def attention_kernel(place_ref, ends_ref, q_hbm, g_hbm, *refs):
    pieces = refs[:PIECES]
    out_hbm, dq_hbm, swap_ref, rest_ref, kv_ref, ones_ref, turned_ref, bias_ref, s_ref, p_ref, acc_ref, *refs = refs[PIECES:]
    q_ref, g_ref, out_ref, dq_ref, sems = refs
    rows = q_ref.shape[0]
    size = kv_ref.shape[1] // 2
    span = kv_ref.shape[0]
    heads = q_ref.shape[1] // size

    arriving = [pltpu.make_async_copy(q_hbm, q_ref, sems.at[0]), pltpu.make_async_copy(g_hbm, g_ref, sems.at[1])]
    leaving = [pltpu.make_async_copy(out_ref, out_hbm, sems.at[2]), pltpu.make_async_copy(dq_ref, dq_hbm, sems.at[3])]
    for copy in arriving:
        copy.start()
    chunks = key_chunks(rows)
    scale = 1.0 / math.sqrt(size)
    scale2 = scale * math.log2(math.e)

    offset, core, ends = place_ref[0], place_ref[1], ends_ref[...]
    position = offset + lax.broadcasted_iota(jnp.int32, (rows, ends.shape[1]), 0)
    start = jnp.max(jnp.where(ends <= position, ends, 0), axis=1, keepdims=True)
    low = start - (offset - SPAN * rows)
    row = lax.broadcasted_iota(jnp.int32, (rows, rows), 0)
    own, second, fourth, other_own, other_second, other_fourth = [piece[...] for piece in pieces]
    first = jnp.where(core == 0, other_second, other_own)
    third = jnp.where(core == 0, other_fourth, other_second)
    for j, piece in enumerate([fourth, third, second, first, own]):
        cols = slice(j * rows, (j + 1) * rows)
        kv_ref[cols, :] = piece
        ones_ref[cols, :size] = piece[:, size:]
        ones_ref[cols, size:] = jnp.ones((rows, size), BF)
        turned_ref[:size, cols] = piece[:, :size].T
        turned_ref[size:, cols] = piece[:, size:].T
        at = lax.broadcasted_iota(jnp.int32, (rows, rows), 1) + j * rows
        allowed = (at >= low) & (at <= row + SPAN * rows)
        bias_ref[:, cols] = jnp.where(allowed, 0.0, NEG)
    acc_ref[...] = jnp.zeros_like(acc_ref)
    for copy in arriving:
        copy.wait()

    def one_head(h):
        lanes = slice(h * size, (h + 1) * size)
        q = q_ref[:, lanes]
        top = jnp.full((rows, size), NEG, F32)
        for c0, c1, r0, r1 in chunks:
            s = mm(q[r0:r1], turned_ref[:size, c0:c1]) + bias_ref[r0:r1, c0:c1]
            s_ref[h % 2, r0:r1, c0:c1] = s
            most = functools.reduce(jnp.maximum, lane_groups(s, size))
            parts = [top[:r0], jnp.maximum(top[r0:r1], most), top[r1:]]
            top = jnp.concatenate([part for part in parts if part.shape[0]], axis=0)
            yield
        peak = jnp.max(top, axis=1, keepdims=True) * scale2
        out = jnp.zeros((rows, 2 * size), F32)
        for c0, c1, r0, r1 in chunks:
            e = jnp.exp2(s_ref[h % 2, r0:r1, c0:c1] * scale2 - peak[r0:r1])
            p = e.astype(BF)
            p_ref[h % 2, r0:r1, c0:c1] = p
            out = onto_rows(out, mm(p, ones_ref[c0:c1, :]), r0, r1)
            yield
        inverse = 1.0 / out[:, size:]
        out = out[:, :size] * inverse
        out_ref[:, lanes] = out.astype(BF)
        scaled = g_ref[:, lanes].astype(F32) * inverse
        g = scaled.astype(BF)
        delta = jnp.sum(g.astype(F32) * out, axis=1, keepdims=True)
        g_turned = scaled.T.astype(BF)
        q_turned = q.astype(F32).T.astype(BF)
        dq = jnp.zeros((rows, size), F32)
        for c0, c1, r0, r1 in chunks:
            p = p_ref[h % 2, r0:r1, c0:c1]
            acc_ref[size:, c0:c1] += mm(g_turned[:, r0:r1], p)
            dp = mm(g[r0:r1], turned_ref[size:, c0:c1]) - delta[r0:r1]
            ds = dp.astype(BF) * p
            dq = onto_rows(dq, mm(ds, kv_ref[c0:c1, :size]), r0, r1)
            acc_ref[:size, c0:c1] += mm(q_turned[:, r0:r1], ds)
            yield
        dq_ref[:, lanes] = (dq * scale).astype(BF)

    running, waiting = [], [one_head(h) for h in range(heads)]
    while running or waiting:
        if waiting:
            running.append(waiting.pop(0))
        for _ in chunks:
            running = [head for head in running if next(head, head) is None]

    for copy in leaving:
        copy.start()
    for j in range(SPAN + 1):
        cols = slice(j * rows, (j + 1) * rows)
        into = rest_ref.at[j // 2] if j % 2 == 0 else swap_ref.at[1 - j // 2]
        into[:, :size] = (acc_ref[:size, cols].T * scale).astype(BF)
        into[:, size:] = acc_ref[size:, cols].T.astype(BF)
    for copy in leaving:
        copy.wait()


def attention(place, ends, queries, out_grad, pieces):
    rows, width = queries.shape
    pair = pieces[0].shape[1]
    size = pair // 2
    heads = width // size
    span = (SPAN + 1) * rows
    far_off = pl.BlockSpec(memory_space=pltpu.HBM)
    near_by = pl.BlockSpec(memory_space=pltpu.VMEM)
    return pl.pallas_call(
        attention_kernel,
        in_specs=[pl.BlockSpec(memory_space=pltpu.SMEM), near_by, far_off, far_off] + [near_by] * PIECES,
        out_specs=[far_off, far_off, near_by, near_by],
        out_shape=[
            jax.ShapeDtypeStruct((rows, width), BF),
            jax.ShapeDtypeStruct((rows, width), BF),
            jax.ShapeDtypeStruct((SPAN // 2, rows, pair), BF),
            jax.ShapeDtypeStruct((SPAN // 2 + 1, rows, pair), BF),
        ],
        scratch_shapes=[
            pltpu.VMEM((span, pair), BF),
            pltpu.VMEM((span, pair), BF),
            pltpu.VMEM((pair, span), BF),
            pltpu.VMEM((rows, span), F32),
            pltpu.VMEM((2, rows, span), F32),
            pltpu.VMEM((2, rows, span), BF),
            pltpu.VMEM((pair, span), F32),
            pltpu.VMEM((rows, width), BF),
            pltpu.VMEM((rows, width), BF),
            pltpu.VMEM((rows, width), BF),
            pltpu.VMEM((rows, width), BF),
            pltpu.SemaphoreType.DMA((4,)),
        ],
        cost_estimate=pl.CostEstimate(
            flops=24 * heads * rows * span * size, bytes_accessed=10 * rows * width, transcendentals=heads * rows * span
        ),
        compiler_params=params(36),
        name="attention",
    )(place, ends, queries, out_grad, *pieces)


def between_cores(block):
    return lax.ppermute(block, "core", SWAP)


def between_chips(block, distance):
    devices = range(lax.axis_size(ALL))
    route = [(i, i + 2 * distance) for i in devices if i + 2 * distance in devices]
    return lax.ppermute(block, ALL, route)


def window_pieces(key_value):
    second = between_chips(key_value, 1)
    fourth = between_chips(key_value, 2)
    mine = [key_value, second, fourth]
    return mine + [between_cores(block) for block in mine]


def returned(swap, rest, core):
    came = between_cores(swap)
    first, third = came[0].astype(F32), came[1].astype(F32)
    near = (rest[1].astype(F32) + jnp.where(core == 0, third, first)).astype(BF)
    far = (rest[0].astype(F32) + jnp.where(core == 0, 0.0, third)).astype(BF)
    own = rest[2].astype(F32) + jnp.where(core == 0, first, 0.0)
    terms = [own, between_chips(near, -1), between_chips(far, -2)]
    return terms + [between_cores(term) for term in terms]


def per_device(hidden, kv_weight, queries, out_grad, lengths):
    rows = hidden.shape[0]
    part, pair = kv_weight.shape
    core = lax.axis_index("core")
    chips = lax.axis_size(CHIPS)

    copies = jnp.broadcast_to(kv_weight[None], (chips, part, pair))
    weight = lax.all_to_all(copies, CHIPS, 0, 0, tiled=True).reshape(chips * part, pair)

    away = picker(1 - core, part)
    came = [between_cores(picked_columns(hidden, away, n, CHUNKS)) for n in range(CHUNKS)]
    keep = picked_columns(hidden, picker(core, part), 0, 1)

    place = jnp.stack([lax.axis_index(ALL) * rows, core]).astype(jnp.int32)
    ends = jnp.cumsum(lengths).astype(jnp.int32)[None, :]

    place, ends, keep = lax.optimization_barrier((place, ends, keep))
    partner = between_cores(projected(came, weight))
    key_value = (mm(keep, weight) + partner).astype(BF)
    pieces = window_pieces(key_value)

    attended, query_grad, swap, rest = attention(place, ends, queries, out_grad, pieces)
    share = chip_share(keep, came, returned(swap, rest, core)).reshape(chips, part, pair)
    spread = lax.all_to_all(share, CHIPS, 0, 0, tiled=True)
    return attended, query_grad, jnp.sum(spread.astype(F32), axis=0)


def solution(mesh):
    cuts, dp = mesh.devices.shape
    fine = Mesh(mesh.devices.reshape(cuts, 4, dp // 8, 2), ALL)
    rows = P(ALL, None)
    return jax.shard_map(
        per_device,
        mesh=fine,
        in_specs=(rows, rows, rows, rows, P()),
        out_specs=(rows, rows, rows),
        check_vma=False,
    )
```
